768 devices in a mesh: blk: 32 (over y, z_hi), rep: 24 (over x, z_lo, core).
Axes of the slice: x: 4, y: 8, z: 12 (z_hi: 4, z_lo: 3; z = z_hi * 3 + z_lo), core: 2. Of those that a mesh axis runs over, the one named last changes fastest.
Arguments:
- tokens: bfloat16 [98304, 8192], P(('blk', 'rep')), may hold values from -6 to 6
- gate_weight: bfloat16 [32, 8192], P('blk'), may hold values from -0.0625 to 0.0625
- up_weight: bfloat16 [32, 8192], P('blk'), may hold values from -0.0625 to 0.0625
- down_weight: bfloat16 [32, 8192], P('blk'), may hold values from -1 to 1
Outputs:
- grad_gate: float32 [32, 8192], P('blk')
- grad_up: float32 [32, 8192], P('blk')
- grad_down: float32 [32, 8192], P('blk')
The draws below stay inside these ranges and needn't reach their ends.
All inputs are finite; a program needn't handle non-finite values.
Results may differ from the reference program's by a relative error of at most 0.0027.
Values may be sent and summed in bfloat16 or wider, within the bound.
No kernel may reach another device: no remote copies, remote signals or barrier semaphores. Data moves between devices by JAX's collectives and lax.ppermute only.
A program may use at most 32 MiB of HBM per device.

```python
import math
import jax
import jax.numpy as jnp
from jax import lax

D = 8192
HIDW = 32
TOKENS = 98304


def steps_of(stream_key, dims, shards, low, largest):
    loudness, own = 1.0, jax.random.fold_in(stream_key, 6)
    for axis_at, parts in shards:
        heights = jnp.exp(jax.random.uniform(jax.random.fold_in(own, axis_at), (parts,), jnp.float32, low / len(shards), largest / len(shards)))
        loudness = loudness * jnp.repeat(heights, dims[axis_at] // parts).reshape([-1 if axis == axis_at else 1 for axis in range(len(dims))])
    return loudness


def gaussian(stream_key, shape, scale, most, shards=(), held_as=jnp.bfloat16):
    drawn = scale * jax.random.normal(stream_key, shape, jnp.float32)
    if shards:
        drawn = drawn * steps_of(stream_key, shape, shards, -0.22, 0.18)
    return jnp.clip(drawn, -most, most).astype(held_as)


def setup_inputs(seed: int = 0) -> dict:
    arg_keys = jax.random.split(jax.random.key(seed), 5)
    tokens = gaussian(arg_keys[0], (TOKENS, D), 1.0, 6.0, ((0, 768),))
    gate_weight = gaussian(arg_keys[1], (HIDW, D), D ** -0.5, 0.0625, ((0, 32),))
    up_weight = gaussian(arg_keys[2], (HIDW, D), D ** -0.5, 0.0625, ((0, 32),))
    down_weight = gaussian(arg_keys[3], (HIDW, D), HIDW ** -0.5, 1.0, ((0, 32),))
    return {"tokens": tokens, "gate_weight": gate_weight, "up_weight": up_weight, "down_weight": down_weight}


def reference(tokens, gate_weight, up_weight, down_weight):
    loss_scale = float(TOKENS) ** -0.5
    block_rows = math.gcd(TOKENS, 2048)
    blocked = tokens.reshape(TOKENS // block_rows, block_rows, D)

    def accumulate(totals, rows):
        gate_pre = jnp.dot(rows, gate_weight.T, preferred_element_type=jnp.float32)
        up_pre = jnp.dot(rows, up_weight.T, preferred_element_type=jnp.float32)
        sigmoid_gate = jax.nn.sigmoid(gate_pre)
        active = gate_pre * sigmoid_gate
        hidden = (active * up_pre).astype(jnp.bfloat16)
        layer_out = jnp.dot(hidden, down_weight, preferred_element_type=jnp.float32)
        cotangent = (layer_out * loss_scale).astype(jnp.bfloat16)
        hidden_grad = jnp.dot(cotangent, down_weight.T, preferred_element_type=jnp.float32)
        gate_grad = (hidden_grad * up_pre * (sigmoid_gate * (1.0 + gate_pre * (1.0 - sigmoid_gate)))).astype(jnp.bfloat16)
        up_grad = (hidden_grad * active).astype(jnp.bfloat16)
        new_gate = totals[0] + jnp.dot(gate_grad.T, rows, preferred_element_type=jnp.float32)
        new_up = totals[1] + jnp.dot(up_grad.T, rows, preferred_element_type=jnp.float32)
        new_down = totals[2] + jnp.dot(hidden.T, cotangent, preferred_element_type=jnp.float32)
        return (new_gate, new_up, new_down), None

    zeros = jnp.zeros((HIDW, D), jnp.float32)
    totals, unused = lax.scan(accumulate, (zeros, zeros, zeros), blocked)
    return (totals[0], totals[1], totals[2])
```

```python
import jax
import jax.numpy as jnp
from jax import lax
from jax.experimental import pallas as pl
from jax.experimental.pallas import tpu as pltpu
from jax.sharding import Mesh
from jax.sharding import PartitionSpec as P

BLK = ("y", "zh")
Z = ("zh", "zl")
REP = ("x", "zl", "c")
NT = (((1,), (1,)), ((), ()))


def sent_to_all(x, axis):
    peers = lax.axis_size(axis)
    return lax.all_to_all(jnp.broadcast_to(x[None], (peers, *x.shape)), axis, 0, 0, tiled=True)


def layer_kernel(loss_scale, core_ref, tok_ref, own_ref, oth_ref, keep_ref, send_ref, cot_ref):
    parts, rows, width = own_ref.shape
    hid = rows // 3
    half = parts * width
    core = core_ref[0]

    def columns(which, part):
        side = core if which == 0 else 1 - core
        return pl.ds(pl.multiple_of(side * half + part * width, width), width)

    pieces = [(which, part) for which in range(2) for part in range(parts)]
    held = (own_ref, oth_ref)
    out = (keep_ref, send_ref)
    pre = jnp.zeros((tok_ref.shape[0], 2 * hid), jnp.float32)
    for which, part in pieces:
        pre += lax.dot_general(
            tok_ref[:, columns(which, part)],
            held[which][part, : 2 * hid, :],
            NT,
            preferred_element_type=jnp.float32,
        )
    gate_pre = pre[:, :hid]
    up_pre = pre[:, hid:]
    sigmoid_gate = jax.nn.sigmoid(gate_pre)
    active = gate_pre * sigmoid_gate
    hidden_wide = (active * up_pre).astype(jnp.bfloat16).astype(jnp.float32)
    hidden = hidden_wide.astype(jnp.bfloat16)
    hidden_t = hidden_wide.T.astype(jnp.bfloat16)
    hidden_grad = jnp.zeros(gate_pre.shape, jnp.float32)
    for which, part in pieces:
        down = held[which][part, 2 * hid :, :]
        layer_out = jnp.dot(hidden, down, preferred_element_type=jnp.float32)
        cotangent = (layer_out * loss_scale).astype(jnp.bfloat16)
        cot_ref[which * parts + part] = cotangent
        hidden_grad += lax.dot_general(cotangent, down, NT, preferred_element_type=jnp.float32)
    gate_grad = hidden_grad * up_pre * (sigmoid_gate * (1.0 + gate_pre * (1.0 - sigmoid_gate)))
    up_grad = hidden_grad * active
    grads_t = jnp.concatenate([gate_grad, up_grad], axis=1).T.astype(jnp.bfloat16)
    for which, part in pieces[parts:] + pieces[:parts]:
        out[which][part, : 2 * hid, :] = jnp.dot(
            grads_t, tok_ref[:, columns(which, part)], preferred_element_type=jnp.float32
        )
        out[which][part, 2 * hid :, :] = jnp.dot(
            hidden_t, cot_ref[which * parts + part], preferred_element_type=jnp.float32
        )


def per_device(tokens, gate_weight, up_weight, down_weight):
    ys, zhs, xs, zls, cs = (lax.axis_size(a) for a in ("y", "zh", "x", "zl", "c"))
    tok_rows, features = tokens.shape
    devices = ys * zhs * xs * zls * cs
    loss_scale = float(tok_rows * devices) ** (-0.5)
    width = features // (xs * cs)
    rows = 3 * ys * zhs
    core = lax.axis_index("c")
    swap = [(i, (i + 1) % cs) for i in range(cs)]

    at = (core * xs + lax.axis_index("x")) * width
    mine = lax.select_n(lax.axis_index("zl"), gate_weight, up_weight, down_weight)
    piece = lax.dynamic_slice(mine, (0, at), (1, width))
    over_z = sent_to_all(piece[0], Z)
    over_y = sent_to_all(over_z, "y").reshape(ys, zhs, zls, width)
    plane = over_y.transpose(2, 0, 1, 3).reshape(rows, width)
    own = sent_to_all(plane, "x")
    other = lax.ppermute(own, "c", swap)

    vmem = pl.BlockSpec(memory_space=pltpu.VMEM)
    term = jax.ShapeDtypeStruct(own.shape, jnp.float32)
    keep, send = pl.pallas_call(
        lambda *refs: layer_kernel(loss_scale, *refs),
        out_shape=(term, term),
        in_specs=[pl.BlockSpec(memory_space=pltpu.SMEM), vmem, vmem, vmem],
        out_specs=(vmem, vmem),
        scratch_shapes=[pltpu.VMEM((cs * xs, tok_rows, width), jnp.bfloat16)],
        compiler_params=pltpu.CompilerParams(vmem_limit_bytes=32 << 20),
        name="layer",
    )(core.reshape(1), tokens, own, other)

    both = (keep + lax.ppermute(send, "c", swap)).astype(jnp.bfloat16)
    got = lax.all_to_all(both, "x", 0, 0, tiled=True)
    sum_x = got.astype(jnp.float32).sum(axis=0).astype(jnp.bfloat16)
    by_y = sum_x.reshape(zls, ys, zhs, width).transpose(1, 2, 0, 3).reshape(ys, zhs * zls, width)
    got = lax.all_to_all(by_y, "y", 0, 0, tiled=True)
    sum_y = got.astype(jnp.float32).sum(axis=0)
    got = lax.all_to_all(sum_y, Z, 0, 0, tiled=True)
    total = got.sum(axis=0)
    every = sent_to_all(total, REP).reshape(xs, zls, cs, width)
    result = every.transpose(1, 2, 0, 3).reshape(zls, 1, features)
    return (result[0], result[1], result[2])


def solution(mesh):
    shape = (8, 4, 4, 3, 2)
    split = Mesh(mesh.devices.reshape(shape), ("y", "zh", "x", "zl", "c"))
    return jax.shard_map(
        per_device,
        mesh=split,
        in_specs=(P(BLK + REP, None), P(BLK, None), P(BLK, None), P(BLK, None)),
        out_specs=(P(BLK, None), P(BLK, None), P(BLK, None)),
        check_vma=False,
    )
```

```python
import jax
import jax.numpy as jnp
from jax import lax
from jax.experimental import pallas as pl
from jax.experimental.pallas import tpu as pltpu
from jax.sharding import Mesh
from jax.sharding import PartitionSpec as P

BLK = ("y", "zh")
REP = ("x", "zl", "c")
PLANE = ("zl", "y", "zh")
OWNERS = ("zl", "c", "x")
TILE = (8, 128)
NT = (((1,), (1,)), ((), ()))


def sent_to_all(x, axis):
    peers = lax.axis_size(axis)
    return lax.all_to_all(jnp.broadcast_to(x[None], (peers, *x.shape)), axis, 0, 0, tiled=True)


def layer_kernel(loss_scale, core_ref, tok_ref, own_ref, oth_ref, keep_ref, send_ref, cot_ref):
    parts, rows, width = own_ref.shape
    hid = rows // 3
    half = parts * width
    core = core_ref[0]

    def columns(which, part):
        side = core if which == 0 else 1 - core
        return pl.ds(pl.multiple_of(side * half + part * width, width), width)

    pieces = [(which, part) for which in range(2) for part in range(parts)]
    held = (own_ref, oth_ref)
    out = (keep_ref, send_ref)
    pre = jnp.zeros((tok_ref.shape[0], 2 * hid), jnp.float32)
    for which, part in pieces:
        pre += lax.dot_general(
            tok_ref[:, columns(which, part)],
            held[which][part, : 2 * hid, :],
            NT,
            preferred_element_type=jnp.float32,
        )
    gate_pre = pre[:, :hid]
    up_pre = pre[:, hid:]
    sigmoid_gate = jax.nn.sigmoid(gate_pre)
    active = gate_pre * sigmoid_gate
    hidden_wide = (active * up_pre).astype(jnp.bfloat16).astype(jnp.float32)
    hidden = hidden_wide.astype(jnp.bfloat16)
    hidden_t = hidden_wide.T.astype(jnp.bfloat16)
    hidden_grad = jnp.zeros(gate_pre.shape, jnp.float32)
    for which, part in pieces:
        down = held[which][part, 2 * hid :, :]
        layer_out = jnp.dot(hidden, down, preferred_element_type=jnp.float32)
        cotangent = (layer_out * loss_scale).astype(jnp.bfloat16)
        cot_ref[which * parts + part] = cotangent
        hidden_grad += lax.dot_general(cotangent, down, NT, preferred_element_type=jnp.float32)
    gate_grad = hidden_grad * up_pre * (sigmoid_gate * (1.0 + gate_pre * (1.0 - sigmoid_gate)))
    up_grad = hidden_grad * active
    grads_t = jnp.concatenate([gate_grad, up_grad], axis=1).T.astype(jnp.bfloat16)
    for which, part in pieces[parts:] + pieces[:parts]:
        out[which][part, : 2 * hid, :] = jnp.dot(
            grads_t, tok_ref[:, columns(which, part)], preferred_element_type=jnp.float32
        )
        out[which][part, 2 * hid :, :] = jnp.dot(
            hidden_t, cot_ref[which * parts + part], preferred_element_type=jnp.float32
        )


def per_device(tokens, gate_weight, up_weight, down_weight):
    ys, zhs, xs, zls, cs = (lax.axis_size(a) for a in ("y", "zh", "x", "zl", "c"))
    tok_rows, features = tokens.shape
    devices = ys * zhs * xs * zls * cs
    loss_scale = float(tok_rows * devices) ** (-0.5)
    width = features // (xs * cs)
    rows = 3 * ys * zhs
    core = lax.axis_index("c")
    swap = [(i, (i + 1) % cs) for i in range(cs)]

    at = (core * xs + lax.axis_index("x")) * width
    mine = lax.select_n(lax.axis_index("zl"), gate_weight, up_weight, down_weight)
    piece = lax.dynamic_slice(mine, (0, at), (1, width)).reshape(TILE)
    plane = sent_to_all(piece, PLANE).reshape(rows, width)
    own = sent_to_all(plane, "x")
    other = lax.ppermute(own, "c", swap)

    vmem = pl.BlockSpec(memory_space=pltpu.VMEM)
    term = jax.ShapeDtypeStruct(own.shape, jnp.float32)
    keep, send = pl.pallas_call(
        lambda *refs: layer_kernel(loss_scale, *refs),
        out_shape=(term, term),
        in_specs=[pl.BlockSpec(memory_space=pltpu.SMEM), vmem, vmem, vmem],
        out_specs=(vmem, vmem),
        scratch_shapes=[pltpu.VMEM((cs * xs, tok_rows, width), jnp.bfloat16)],
        compiler_params=pltpu.CompilerParams(vmem_limit_bytes=32 << 20),
        name="layer",
    )(core.reshape(1), tokens, own, other)

    both = (keep + lax.ppermute(send, "c", swap)).astype(jnp.bfloat16)
    got = lax.all_to_all(both, "x", 0, 0, tiled=True)
    sum_x = got.astype(jnp.float32).sum(axis=0).astype(jnp.bfloat16)
    got = lax.all_to_all(sum_x.reshape(rows, *TILE), PLANE, 0, 0, tiled=True)
    total = got.astype(jnp.float32).sum(axis=0)
    result = sent_to_all(total, OWNERS).reshape(zls, 1, features)
    return (result[0], result[1], result[2])


def solution(mesh):
    shape = (8, 4, 4, 3, 2)
    split = Mesh(mesh.devices.reshape(shape), ("y", "zh", "x", "zl", "c"))
    return jax.shard_map(
        per_device,
        mesh=split,
        in_specs=(P(BLK + REP, None), P(BLK, None), P(BLK, None), P(BLK, None)),
        out_specs=(P(BLK, None), P(BLK, None), P(BLK, None)),
        check_vma=False,
    )
```

```python
import jax
import jax.numpy as jnp
from jax import lax
from jax.experimental import pallas as pl
from jax.experimental.pallas import tpu as pltpu
from jax.sharding import Mesh
from jax.sharding import PartitionSpec as P

BLK = ("y", "zh")
REP = ("x", "zl", "c")
PLANE = ("zl", "y", "zh")
OWNERS = ("zl", "c", "x")
ROW_TILE = (8, 128)
HIGH, LANES = 16, 128
NT = (((1,), (1,)), ((), ()))
F32, BF16 = jnp.float32, jnp.bfloat16


def sent_to_all(x, axis):
    peers = lax.axis_size(axis)
    return lax.all_to_all(jnp.broadcast_to(x[None], (peers, *x.shape)), axis, 0, 0, tiled=True)


def halves(square):
    high = square.astype(BF16).astype(F32)
    return high, (square - high).astype(BF16).astype(F32)


def square_to_tile(square):
    n = square.shape[0]
    high, low = halves(square)
    parts = []
    for at in range(0, n, HIGH):
        parts += [high[at : at + HIGH], low[at : at + HIGH]]
    if (spare := LANES - 2 * n * (n // HIGH)) > 0:
        parts.append(jnp.zeros((HIGH, spare), F32))
    return jnp.concatenate(parts, axis=1).astype(BF16)


def tile_to_square(tile, n):
    wide = tile.astype(F32)
    rows = []
    for group in range(n // HIGH):
        at = 2 * n * group
        rows.append(wide[:, at : at + n] + wide[:, at + n : at + 2 * n])
    return jnp.concatenate(rows, axis=0)


def places(rows, width):
    return [
        (slice(r, r + HIGH), slice(c, c + LANES))
        for r in range(0, rows, HIGH)
        for c in range(0, width, LANES)
    ]


def from_tiles(ref, part, rows, width):
    across = width // LANES
    return jnp.concatenate(
        [
            jnp.concatenate([ref[part, r * across + c] for c in range(across)], axis=1)
            for r in range(rows // HIGH)
        ],
        axis=0,
    )


def pack_kernel(plane_ref, out_ref):
    rows, width = plane_ref.shape
    two = 2 * rows // 3
    peers = out_ref.shape[0]
    down = plane_ref[two:, :]
    square = square_to_tile(lax.dot_general(down, down, NT, preferred_element_type=F32))
    for at, (r, c) in enumerate(places(two, width)):
        tile = plane_ref[r, c]
        for p in range(peers):
            out_ref[p, at] = tile
    for p in range(peers):
        out_ref[p, out_ref.shape[1] - 1] = square


def token_columns(core, part, tok_ref, got_ref, parts):
    width = got_ref.shape[1] // parts
    own = tok_ref[:, pl.ds(pl.multiple_of(core * got_ref.shape[1] + part * width, width), width)]
    return jnp.concatenate([own, got_ref[:, part * width : (part + 1) * width]], axis=0)


def pre_kernel(core_ref, tok_ref, got_ref, w_ref, out_ref):
    parts, tiles = w_ref.shape[:2]
    width = got_ref.shape[1] // parts
    two = (tiles - 1) * HIGH * LANES // width
    hid = two // 2
    core = core_ref[0]
    pre = jnp.zeros((2 * tok_ref.shape[0], two), F32)
    square = jnp.zeros((hid, hid), F32)
    for part in range(parts):
        pre += lax.dot_general(
            token_columns(core, part, tok_ref, got_ref, parts),
            from_tiles(w_ref, part, two, width),
            NT,
            preferred_element_type=F32,
        )
        square += tile_to_square(w_ref[part, tiles - 1], hid)
    out_ref[:two, :] = pre.T
    blank = jnp.zeros((hid, out_ref.shape[1] - hid), F32)
    out_ref[two:, :] = jnp.concatenate([square, blank], axis=1)


def grad_kernel(loss_scale, core_ref, tok_ref, got_ref, own_ref, other_ref, out_ref):
    parts, tiles = out_ref.shape[:2]
    width = got_ref.shape[1] // parts
    two = (tiles - 1) * HIGH * LANES // width
    hid = two // 2
    toks = tok_ref.shape[0]
    core = core_ref[0]
    other = jnp.concatenate([other_ref[:two, toks:], other_ref[:two, :toks]], axis=1)
    pre = own_ref[:two, :] + other
    high, low = halves(own_ref[two:, :hid] + other_ref[two:, :hid])
    gate_pre = pre[:hid]
    up_pre = pre[hid:]
    sigmoid_gate = jax.nn.sigmoid(gate_pre)
    active = gate_pre * sigmoid_gate
    hidden = (active * up_pre).astype(BF16)
    hidden_grad = loss_scale * (
        jnp.dot(high.astype(BF16), hidden, preferred_element_type=F32)
        + jnp.dot(low.astype(BF16), hidden, preferred_element_type=F32)
    )
    gate_grad = hidden_grad * up_pre * (sigmoid_gate * (1.0 + gate_pre * (1.0 - sigmoid_gate)))
    up_grad = hidden_grad * active
    grads = jnp.concatenate([gate_grad, up_grad], axis=0).astype(BF16)
    square = square_to_tile(lax.dot_general(hidden, hidden, NT, preferred_element_type=F32))
    for part in range(parts):
        terms = jnp.dot(
            grads,
            token_columns(core, part, tok_ref, got_ref, parts),
            preferred_element_type=F32,
        ).astype(BF16)
        for at, (r, c) in enumerate(places(two, width)):
            out_ref[part, at] = terms[r, c]
        out_ref[part, tiles - 1] = square


def sum_kernel(got_ref, out_ref):
    parts, tiles = got_ref.shape[:2]
    rows, width = out_ref.shape
    two = 2 * rows // 3
    hid = two // 2
    for at, (r, c) in enumerate(places(two, width)):
        total = got_ref[0, at].astype(F32)
        for p in range(1, parts):
            total += got_ref[p, at].astype(F32)
        out_ref[r, c] = total.astype(BF16)
    square = tile_to_square(got_ref[0, tiles - 1], hid)
    for p in range(1, parts):
        square += tile_to_square(got_ref[p, tiles - 1], hid)
    blank = jnp.zeros((hid, LANES - hid), F32)
    high, low = halves(square)
    both = [jnp.concatenate([half, blank], axis=1).astype(BF16) for half in (high, low)]
    out_ref[two:, : 2 * LANES] = jnp.concatenate(both, axis=1)
    out_ref[two:, 2 * LANES :] = jnp.zeros((hid, width - 2 * LANES), BF16)


def final_kernel(loss_scale, kind_ref, got_ref, gathered_ref, out_ref):
    total = got_ref[0].astype(F32)
    for at in range(1, got_ref.shape[0]):
        total += got_ref[at].astype(F32)
    hid = gathered_ref.shape[0] // 3

    @pl.when(kind_ref[0] != 2)
    def _():
        for to in range(out_ref.shape[0]):
            out_ref[to] = total

    @pl.when(kind_ref[0] == 2)
    def _():
        row = (total[0:1] + total[1:2]) * loss_scale
        result = jnp.zeros(total.shape, F32)
        for at in range(hid):
            factor = jnp.broadcast_to(row[:, at : at + 1], total.shape)
            result += factor * gathered_ref[2 * hid + at].astype(F32)
        for to in range(out_ref.shape[0]):
            out_ref[to] = result


def call(kernel, name, shape, dtype, *args):
    vmem = pl.BlockSpec(memory_space=pltpu.VMEM)
    smem = pl.BlockSpec(memory_space=pltpu.SMEM)
    return pl.pallas_call(
        kernel,
        out_shape=jax.ShapeDtypeStruct(shape, dtype),
        in_specs=[smem if a.dtype == jnp.int32 else vmem for a in args],
        out_specs=vmem,
        compiler_params=pltpu.CompilerParams(vmem_limit_bytes=32 << 20),
        name=name,
    )(*args)


def per_device(tokens, gate_weight, up_weight, down_weight):
    ys, zhs, xs, zls, cs = (lax.axis_size(a) for a in ("y", "zh", "x", "zl", "c"))
    tok_rows, features = tokens.shape
    devices = ys * zhs * xs * zls * cs
    loss_scale = float(tok_rows * devices) ** (-0.5)
    width = features // (xs * cs)
    rows = 3 * ys * zhs
    two = 2 * rows // 3
    tiles = two * width // (HIGH * LANES) + 1
    core = lax.axis_index("c")
    kind = lax.axis_index("zl")
    swap = [(i, (i + 1) % cs) for i in range(cs)]
    side = features // cs

    sent = lax.dynamic_slice(tokens, (0, (1 - core) * side), (tok_rows, side))
    got_tokens = lax.ppermute(sent, "c", swap)

    at = (core * xs + lax.axis_index("x")) * width
    mine = lax.select_n(kind, gate_weight, up_weight, down_weight)
    piece = lax.dynamic_slice(mine, (0, at), (1, width)).reshape(ROW_TILE)
    gathered = sent_to_all(piece, PLANE)
    packed = call(
        pack_kernel, "pack", (xs, tiles, HIGH, LANES), BF16, gathered.reshape(rows, width)
    )
    weights = lax.all_to_all(packed, "x", 0, 0, tiled=True)

    which = core.reshape(1)
    pre = call(
        pre_kernel, "pre", (rows, cs * tok_rows), F32, which, tokens, got_tokens, weights
    )
    other = lax.ppermute(pre, "c", swap)
    terms = call(
        lambda *refs: grad_kernel(loss_scale, *refs),
        "grad",
        (xs, tiles, HIGH, LANES),
        BF16,
        which,
        tokens,
        got_tokens,
        pre,
        other,
    )
    got = lax.all_to_all(terms, "x", 0, 0, tiled=True)
    sums = call(sum_kernel, "sums", (rows, width), BF16, got)
    got = lax.all_to_all(sums.reshape(rows, *ROW_TILE), PLANE, 0, 0, tiled=True)
    every = call(
        lambda *refs: final_kernel(loss_scale, *refs),
        "final",
        (xs * zls * cs, *ROW_TILE),
        F32,
        kind.reshape(1),
        got,
        gathered,
    )
    result = lax.all_to_all(every, OWNERS, 0, 0, tiled=True).reshape(zls, 1, features)
    return (result[0], result[1], result[2])


def split_mesh(mesh, shape):
    return Mesh(mesh.devices.reshape(shape), ("y", "zh", "x", "zl", "c"))


def solution(mesh):
    return jax.shard_map(
        per_device,
        mesh=split_mesh(mesh, (8, 4, 4, 3, 2)),
        in_specs=(P(BLK + REP, None), P(BLK, None), P(BLK, None), P(BLK, None)),
        out_specs=(P(BLK, None), P(BLK, None), P(BLK, None)),
        check_vma=False,
    )
```

```python
import jax
import jax.numpy as jnp
from jax import lax
from jax.experimental import pallas as pl
from jax.experimental.pallas import tpu as pltpu
from jax.sharding import Mesh
from jax.sharding import PartitionSpec as P

AXES = ("yh", "yl", "zh", "x", "zl", "c")
BLK = AXES[:3]
PLANE = ("zl", "yl", "yh", "zh")
NEAR = ("x", "yl")
FAR = ("zl", "yh", "zh")
OWNERS = ("zl", "c", "x")
ROW_TILE = (8, 128)
HIGH, LANES = 16, 128
NT = (((1,), (1,)), ((), ()))
F32, BF16 = jnp.float32, jnp.bfloat16
VMEM = pl.BlockSpec(memory_space=pltpu.VMEM)
SMEM = pl.BlockSpec(memory_space=pltpu.SMEM)


def sent_to_all(x, axis):
    peers = lax.axis_size(axis)
    return lax.all_to_all(jnp.broadcast_to(x[None], (peers, *x.shape)), axis, 0, 0, tiled=True)


def halves(square):
    high = square.astype(BF16).astype(F32)
    return high, (square - high).astype(BF16).astype(F32)


def square_to_tile(square):
    m, n = square.shape
    high, low = halves(square)
    parts = []
    for at in range(0, m, HIGH):
        parts += [high[at : at + HIGH], low[at : at + HIGH]]
    if (spare := LANES - 2 * n * (m // HIGH)) > 0:
        parts.append(jnp.zeros((HIGH, spare), F32))
    return jnp.concatenate(parts, axis=1).astype(BF16)


def tile_to_square(tile, m, n):
    wide = tile.astype(F32)
    rows = []
    for group in range(m // HIGH):
        at = 2 * n * group
        rows.append(wide[:, at : at + n] + wide[:, at + n : at + 2 * n])
    return jnp.concatenate(rows, axis=0)


def places(rows, width):
    return [
        (slice(r, r + HIGH), slice(c, c + LANES))
        for r in range(0, rows, HIGH)
        for c in range(0, width, LANES)
    ]


def from_tiles(ref, part, rows, width):
    across = width // LANES
    return jnp.concatenate(
        [
            jnp.concatenate([ref[part, r * across + c] for c in range(across)], axis=1)
            for r in range(rows // HIGH)
        ],
        axis=0,
    )


def pack_kernel(plane_ref, out_ref):
    rows, width = plane_ref.shape
    two = 2 * rows // 3
    peers = out_ref.shape[0]
    down = plane_ref[two:, :]
    square = square_to_tile(lax.dot_general(down, down, NT, preferred_element_type=F32))
    for at, (r, c) in enumerate(places(two, width)):
        tile = plane_ref[r, c]
        for p in range(peers):
            out_ref[p, at] = tile
    for p in range(peers):
        out_ref[p, out_ref.shape[1] - 1] = square


def own_columns(core, part, parts, width):
    return pl.ds(pl.multiple_of((core * parts + part) * width, width), width)


def pre_kernel(width, core_ref, tok_ref, got_ref, w_ref, out_ref, half_ref, sem):
    parts, tiles = w_ref.shape[:2]
    two = (tiles - 1) * HIGH * LANES // width
    hid = two // 2
    core = core_ref[0]
    side = half_ref.shape[1]
    copy = pltpu.make_async_copy(
        got_ref.at[:, pl.ds(pl.multiple_of(core * side, side), side)], half_ref, sem
    )
    copy.start()
    weights = [from_tiles(w_ref, part, two, width) for part in range(parts)]
    square = jnp.zeros((hid, hid), F32)
    own = jnp.zeros((tok_ref.shape[0], two), F32)
    for part in range(parts):
        own += lax.dot_general(
            tok_ref[:, own_columns(core, part, parts, width)],
            weights[part],
            NT,
            preferred_element_type=F32,
        )
        square += tile_to_square(w_ref[part, tiles - 1], hid, hid)
    copy.wait()
    other = jnp.zeros((tok_ref.shape[0], two), F32)
    for part in range(parts):
        other += lax.dot_general(
            half_ref[:, part * width : (part + 1) * width],
            weights[part],
            NT,
            preferred_element_type=F32,
        )
    out_ref[:two, :] = jnp.concatenate([own, other], axis=0).T
    blank = jnp.zeros((hid, out_ref.shape[1] - hid), F32)
    out_ref[two:, :] = jnp.concatenate([square, blank], axis=1)


def grad_kernel(loss_scale, width, parts, core_ref, tok_ref, half_ref, own_ref, other_ref, out_ref):
    peers, tiles = out_ref.shape[:2]
    lanes = peers // parts
    hid = own_ref.shape[0] // 3
    two = 2 * hid
    share = hid // lanes
    toks = tok_ref.shape[0]
    core = core_ref[0]
    other = jnp.concatenate([other_ref[:two, toks:], other_ref[:two, :toks]], axis=1)
    pre = own_ref[:two, :] + other
    high, low = halves(own_ref[two:, :hid] + other_ref[two:, :hid])
    gate_pre = pre[:hid]
    up_pre = pre[hid:]
    sigmoid_gate = jax.nn.sigmoid(gate_pre)
    active = gate_pre * sigmoid_gate
    hidden = (active * up_pre).astype(BF16)
    hidden_grad = loss_scale * (
        jnp.dot(high.astype(BF16), hidden, preferred_element_type=F32)
        + jnp.dot(low.astype(BF16), hidden, preferred_element_type=F32)
    )
    gate_grad = hidden_grad * up_pre * (sigmoid_gate * (1.0 + gate_pre * (1.0 - sigmoid_gate)))
    up_grad = hidden_grad * active
    grads = jnp.concatenate([gate_grad, up_grad], axis=0).astype(BF16)
    square = lax.dot_general(hidden, hidden, NT, preferred_element_type=F32)
    squares = [square_to_tile(square[k * share : (k + 1) * share]) for k in range(lanes)]
    for part in range(parts):
        own = tok_ref[:, own_columns(core, part, parts, width)]
        chip = jnp.concatenate([own, half_ref[:, part * width : (part + 1) * width]], axis=0)
        terms = jnp.dot(grads, chip, preferred_element_type=F32).astype(BF16)
        for lane in range(lanes):
            to = part * lanes + lane
            for at, (r, c) in enumerate(places(2 * share, width)):
                which, row = divmod(r.start, share)
                first = which * hid + lane * share + row
                out_ref[to, at] = terms[first : first + HIGH, c]
            out_ref[to, tiles - 1] = squares[lane]


def sum_kernel(hid, got_ref, out_ref):
    peers, tiles = got_ref.shape[:2]
    rows, width = out_ref.shape
    two = 2 * rows // 3
    share = two // 2
    for at, (r, c) in enumerate(places(two, width)):
        total = got_ref[0, at].astype(F32)
        for p in range(1, peers):
            total += got_ref[p, at].astype(F32)
        out_ref[r, c] = total.astype(BF16)
    square = tile_to_square(got_ref[0, tiles - 1], share, hid)
    for p in range(1, peers):
        square += tile_to_square(got_ref[p, tiles - 1], share, hid)
    blank = jnp.zeros((share, LANES - hid), F32)
    high, low = halves(square)
    both = [jnp.concatenate([half, blank], axis=1).astype(BF16) for half in (high, low)]
    out_ref[two:, : 2 * LANES] = jnp.concatenate(both, axis=1)
    out_ref[two:, 2 * LANES :] = jnp.zeros((share, width - 2 * LANES), BF16)


def final_kernel(loss_scale, kind_ref, got_ref, gathered_ref, out_ref):
    total = got_ref[0].astype(F32)
    for at in range(1, got_ref.shape[0]):
        total += got_ref[at].astype(F32)
    hid = gathered_ref.shape[0] // 3

    @pl.when(kind_ref[0] != 2)
    def _():
        for to in range(out_ref.shape[0]):
            out_ref[to] = total

    @pl.when(kind_ref[0] == 2)
    def _():
        row = (total[0:1] + total[1:2]) * loss_scale
        result = jnp.zeros(total.shape, F32)
        for at in range(hid):
            factor = jnp.broadcast_to(row[:, at : at + 1], total.shape)
            result += factor * gathered_ref[2 * hid + at].astype(F32)
        for to in range(out_ref.shape[0]):
            out_ref[to] = result


def call(kernel, name, shape, dtype, *args):
    return pl.pallas_call(
        kernel,
        out_shape=jax.ShapeDtypeStruct(shape, dtype),
        in_specs=[SMEM if a.dtype == jnp.int32 else VMEM for a in args],
        out_specs=VMEM,
        compiler_params=pltpu.CompilerParams(vmem_limit_bytes=32 << 20),
        name=name,
    )(*args)


def per_device(tokens, gate_weight, up_weight, down_weight):
    xs, cs, yls, zls = (lax.axis_size(a) for a in ("x", "c", "yl", "zl"))
    tok_rows, features = tokens.shape
    hid = lax.axis_size(BLK)
    loss_scale = float(tok_rows * lax.axis_size(AXES)) ** (-0.5)
    width = features // (xs * cs)
    rows = 3 * hid
    tiles = 2 * hid * width // (HIGH * LANES)
    core = lax.axis_index("c")
    kind = lax.axis_index("zl")
    swap = [(i, (i + 1) % cs) for i in range(cs)]

    got_tokens = lax.ppermute(tokens, "c", swap)

    at = (core * xs + lax.axis_index("x")) * width
    mine = lax.select_n(kind, gate_weight, up_weight, down_weight)
    piece = lax.dynamic_slice(mine, (0, at), (1, width)).reshape(ROW_TILE)
    gathered = sent_to_all(piece, PLANE)
    packed = call(
        pack_kernel,
        "pack",
        (xs, tiles + 1, HIGH, LANES),
        BF16,
        gathered.reshape(rows, width),
    )
    weights = lax.all_to_all(packed, "x", 0, 0, tiled=True)

    which = core.reshape(1)
    pre, half = pl.pallas_call(
        lambda *refs: pre_kernel(width, *refs),
        out_shape=(
            jax.ShapeDtypeStruct((rows, cs * tok_rows), F32),
            jax.ShapeDtypeStruct((tok_rows, features // cs), BF16),
        ),
        in_specs=[SMEM, VMEM, pl.BlockSpec(memory_space=pl.ANY), VMEM],
        out_specs=(VMEM, VMEM),
        scratch_shapes=[pltpu.SemaphoreType.DMA],
        compiler_params=pltpu.CompilerParams(vmem_limit_bytes=32 << 20),
        name="pre",
    )(which, tokens, got_tokens, weights)
    other = lax.ppermute(pre, "c", swap)
    terms = call(
        lambda *refs: grad_kernel(loss_scale, width, xs, *refs),
        "grad",
        (xs * yls, tiles // yls + 1, HIGH, LANES),
        BF16,
        which,
        tokens,
        half,
        pre,
        other,
    )
    got = lax.all_to_all(terms, NEAR, 0, 0, tiled=True)
    sums = call(lambda *refs: sum_kernel(hid, *refs), "sums", (rows // yls, width), BF16, got)
    got = lax.all_to_all(sums.reshape(-1, *ROW_TILE), FAR, 0, 0, tiled=True)
    every = call(
        lambda *refs: final_kernel(loss_scale, *refs),
        "final",
        (xs * zls * cs, *ROW_TILE),
        F32,
        kind.reshape(1),
        got,
        gathered,
    )
    result = lax.all_to_all(every, OWNERS, 0, 0, tiled=True).reshape(zls, 1, features)
    return (result[0], result[1], result[2])


def solution(mesh):
    split = Mesh(mesh.devices.reshape(4, 2, 4, 4, 3, 2), AXES)
    return jax.shard_map(
        per_device,
        mesh=split,
        in_specs=(P(AXES, None), P(BLK, None), P(BLK, None), P(BLK, None)),
        out_specs=(P(BLK, None), P(BLK, None), P(BLK, None)),
        check_vma=False,
    )
```

```python
import jax
import jax.numpy as jnp
from jax import lax
from jax.experimental import pallas as pl
from jax.experimental.pallas import tpu as pltpu
from jax.sharding import Mesh
from jax.sharding import PartitionSpec as P

AXES = ("yh", "yl", "zh", "x", "zl", "c")
BLK = AXES[:3]
PLANE = ("zl", "yl", "yh", "zh")
NEAR = ("x", "yl")
FAR = ("zl", "yh", "zh")
OWNERS = ("zl", "c", "x")
ROW_TILE = (8, 128)
HIGH, LANES = 16, 128
NT = (((1,), (1,)), ((), ()))
F32, BF16 = jnp.float32, jnp.bfloat16
VMEM = pl.BlockSpec(memory_space=pltpu.VMEM)
SMEM = pl.BlockSpec(memory_space=pltpu.SMEM)


def sent_to_all(x, axis):
    peers = lax.axis_size(axis)
    return lax.all_to_all(jnp.broadcast_to(x[None], (peers, *x.shape)), axis, 0, 0, tiled=True)


def halves(square):
    high = square.astype(BF16).astype(F32)
    return high, (square - high).astype(BF16).astype(F32)


def square_to_tile(square):
    m, n = square.shape
    high, low = halves(square)
    parts = []
    for at in range(0, m, HIGH):
        parts += [high[at : at + HIGH], low[at : at + HIGH]]
    if (spare := LANES - 2 * n * (m // HIGH)) > 0:
        parts.append(jnp.zeros((HIGH, spare), F32))
    return jnp.concatenate(parts, axis=1).astype(BF16)


def tile_to_square(tile, m, n):
    wide = tile.astype(F32)
    rows = []
    for group in range(m // HIGH):
        at = 2 * n * group
        rows.append(wide[:, at : at + n] + wide[:, at + n : at + 2 * n])
    return jnp.concatenate(rows, axis=0)


def places(rows, width):
    return [
        (slice(r, r + HIGH), slice(c, c + LANES))
        for r in range(0, rows, HIGH)
        for c in range(0, width, LANES)
    ]


def from_tiles(ref, part, rows, width):
    across = width // LANES
    return jnp.concatenate(
        [
            jnp.concatenate([ref[part, r * across + c] for c in range(across)], axis=1)
            for r in range(rows // HIGH)
        ],
        axis=0,
    )


def pack_kernel(plane_ref, unused_ref, out_ref):
    rows, width = plane_ref.shape
    two = 2 * rows // 3
    peers = out_ref.shape[0]
    down = plane_ref[two:, :]
    square = square_to_tile(lax.dot_general(down, down, NT, preferred_element_type=F32))
    for at, (r, c) in enumerate(places(two, width)):
        tile = plane_ref[r, c]
        for p in range(peers):
            out_ref[p, at] = tile
    for p in range(peers):
        out_ref[p, out_ref.shape[1] - 1] = square


def token_columns(core, part, parts, width, tok_ref, got_ref):
    columns = pl.ds(pl.multiple_of((core * parts + part) * width, width), width)
    return jnp.concatenate([tok_ref[:, columns], got_ref[:, columns]], axis=0)


def pre_kernel(width, core_ref, tok_ref, got_ref, w_ref, out_ref):
    parts, tiles = w_ref.shape[:2]
    two = (tiles - 1) * HIGH * LANES // width
    hid = two // 2
    core = core_ref[0]
    pre = jnp.zeros((2 * tok_ref.shape[0], two), F32)
    square = jnp.zeros((hid, hid), F32)
    for part in range(parts):
        pre += lax.dot_general(
            token_columns(core, part, parts, width, tok_ref, got_ref),
            from_tiles(w_ref, part, two, width),
            NT,
            preferred_element_type=F32,
        )
        square += tile_to_square(w_ref[part, tiles - 1], hid, hid)
    out_ref[:two, :] = pre.T
    blank = jnp.zeros((hid, out_ref.shape[1] - hid), F32)
    out_ref[two:, :] = jnp.concatenate([square, blank], axis=1)


def grad_kernel(loss_scale, width, parts, core_ref, tok_ref, got_ref, own_ref, other_ref, out_ref):
    peers, tiles = out_ref.shape[:2]
    lanes = peers // parts
    hid = own_ref.shape[0] // 3
    two = 2 * hid
    share = hid // lanes
    toks = tok_ref.shape[0]
    core = core_ref[0]
    other = jnp.concatenate([other_ref[:two, toks:], other_ref[:two, :toks]], axis=1)
    pre = own_ref[:two, :] + other
    high, low = halves(own_ref[two:, :hid] + other_ref[two:, :hid])
    gate_pre = pre[:hid]
    up_pre = pre[hid:]
    sigmoid_gate = jax.nn.sigmoid(gate_pre)
    active = gate_pre * sigmoid_gate
    hidden = (active * up_pre).astype(BF16)
    hidden_grad = loss_scale * (
        jnp.dot(high.astype(BF16), hidden, preferred_element_type=F32)
        + jnp.dot(low.astype(BF16), hidden, preferred_element_type=F32)
    )
    gate_grad = hidden_grad * up_pre * (sigmoid_gate * (1.0 + gate_pre * (1.0 - sigmoid_gate)))
    up_grad = hidden_grad * active
    grads = jnp.concatenate([gate_grad, up_grad], axis=0).astype(BF16)
    square = lax.dot_general(hidden, hidden, NT, preferred_element_type=F32)
    squares = [square_to_tile(square[k * share : (k + 1) * share]) for k in range(lanes)]
    for part in range(parts):
        chip = token_columns(core, part, parts, width, tok_ref, got_ref)
        terms = jnp.dot(grads, chip, preferred_element_type=F32).astype(BF16)
        for lane in range(lanes):
            to = part * lanes + lane
            for at, (r, c) in enumerate(places(2 * share, width)):
                which, row = divmod(r.start, share)
                first = which * hid + lane * share + row
                out_ref[to, at] = terms[first : first + HIGH, c]
            out_ref[to, tiles - 1] = squares[lane]


def sum_kernel(hid, got_ref, out_ref):
    peers, tiles = got_ref.shape[:2]
    rows, width = out_ref.shape
    two = 2 * rows // 3
    share = two // 2
    for at, (r, c) in enumerate(places(two, width)):
        total = got_ref[0, at].astype(F32)
        for p in range(1, peers):
            total += got_ref[p, at].astype(F32)
        out_ref[r, c] = total.astype(BF16)
    square = tile_to_square(got_ref[0, tiles - 1], share, hid)
    for p in range(1, peers):
        square += tile_to_square(got_ref[p, tiles - 1], share, hid)
    blank = jnp.zeros((share, LANES - hid), F32)
    high, low = halves(square)
    both = [jnp.concatenate([half, blank], axis=1).astype(BF16) for half in (high, low)]
    out_ref[two:, : 2 * LANES] = jnp.concatenate(both, axis=1)
    out_ref[two:, 2 * LANES :] = jnp.zeros((share, width - 2 * LANES), BF16)


def final_kernel(loss_scale, kind_ref, got_ref, gathered_ref, out_ref):
    total = got_ref[0].astype(F32)
    for at in range(1, got_ref.shape[0]):
        total += got_ref[at].astype(F32)
    hid = gathered_ref.shape[0] // 3

    @pl.when(kind_ref[0] != 2)
    def _():
        for to in range(out_ref.shape[0]):
            out_ref[to] = total

    @pl.when(kind_ref[0] == 2)
    def _():
        row = (total[0:1] + total[1:2]) * loss_scale
        result = jnp.zeros(total.shape, F32)
        for at in range(hid):
            factor = jnp.broadcast_to(row[:, at : at + 1], total.shape)
            result += factor * gathered_ref[2 * hid + at].astype(F32)
        for to in range(out_ref.shape[0]):
            out_ref[to] = result


def call(kernel, name, shape, dtype, *args):
    return pl.pallas_call(
        kernel,
        out_shape=jax.ShapeDtypeStruct(shape, dtype),
        in_specs=[SMEM if a.dtype == jnp.int32 else VMEM for a in args],
        out_specs=VMEM,
        compiler_params=pltpu.CompilerParams(vmem_limit_bytes=32 << 20),
        name=name,
    )(*args)


def per_device(tokens, gate_weight, up_weight, down_weight):
    xs, cs, yls, zls = (lax.axis_size(a) for a in ("x", "c", "yl", "zl"))
    tok_rows, features = tokens.shape
    hid = lax.axis_size(BLK)
    loss_scale = float(tok_rows * lax.axis_size(AXES)) ** (-0.5)
    width = features // (xs * cs)
    rows = 3 * hid
    tiles = 2 * hid * width // (HIGH * LANES)
    core = lax.axis_index("c")
    kind = lax.axis_index("zl")
    swap = [(i, (i + 1) % cs) for i in range(cs)]

    got_tokens = lax.ppermute(tokens, "c", swap)

    at = (core * xs + lax.axis_index("x")) * width
    mine = lax.select_n(kind, gate_weight, up_weight, down_weight)
    piece = lax.dynamic_slice(mine, (0, at), (1, width)).reshape(ROW_TILE)
    gathered = sent_to_all(piece, PLANE)
    packed = pl.pallas_call(
        pack_kernel,
        out_shape=jax.ShapeDtypeStruct((xs, tiles + 1, HIGH, LANES), BF16),
        in_specs=[VMEM, pl.BlockSpec(memory_space=pl.ANY)],
        out_specs=VMEM,
        compiler_params=pltpu.CompilerParams(vmem_limit_bytes=32 << 20),
        name="pack",
    )(gathered.reshape(rows, width), got_tokens)
    weights = lax.all_to_all(packed, "x", 0, 0, tiled=True)

    which = core.reshape(1)
    pre = call(
        lambda *refs: pre_kernel(width, *refs),
        "pre",
        (rows, cs * tok_rows),
        F32,
        which,
        tokens,
        got_tokens,
        weights,
    )
    other = lax.ppermute(pre, "c", swap)
    terms = call(
        lambda *refs: grad_kernel(loss_scale, width, xs, *refs),
        "grad",
        (xs * yls, tiles // yls + 1, HIGH, LANES),
        BF16,
        which,
        tokens,
        got_tokens,
        pre,
        other,
    )
    got = lax.all_to_all(terms, NEAR, 0, 0, tiled=True)
    sums = call(lambda *refs: sum_kernel(hid, *refs), "sums", (rows // yls, width), BF16, got)
    got = lax.all_to_all(sums.reshape(-1, *ROW_TILE), FAR, 0, 0, tiled=True)
    every = call(
        lambda *refs: final_kernel(loss_scale, *refs),
        "final",
        (xs * zls * cs, *ROW_TILE),
        F32,
        kind.reshape(1),
        got,
        gathered,
    )
    result = lax.all_to_all(every, OWNERS, 0, 0, tiled=True).reshape(zls, 1, features)
    return (result[0], result[1], result[2])


def solution(mesh):
    split = Mesh(mesh.devices.reshape(4, 2, 4, 4, 3, 2), AXES)
    return jax.shard_map(
        per_device,
        mesh=split,
        in_specs=(P(AXES, None), P(BLK, None), P(BLK, None), P(BLK, None)),
        out_specs=(P(BLK, None), P(BLK, None), P(BLK, None)),
        check_vma=False,
    )
```

```python
import jax
import jax.numpy as jnp
from jax import lax
from jax.experimental import pallas as pl
from jax.experimental.pallas import tpu as pltpu
from jax.sharding import Mesh
from jax.sharding import PartitionSpec as P

AXES = ("yh", "yl", "zh", "x", "zl", "c")
BLK = AXES[:3]
PLANE = ("yh", "yl", "zh", "zl")
NEAR = ("x", "yl")
FAR = ("yh", "zh", "zl")
OWNERS = ("zl", "c", "x")
ROW_TILE = (8, 128)
HIGH, LANES = 16, 128
NT = (((1,), (1,)), ((), ()))
F32, BF16 = jnp.float32, jnp.bfloat16
VMEM = pl.BlockSpec(memory_space=pltpu.VMEM)
SMEM = pl.BlockSpec(memory_space=pltpu.SMEM)


def sent_to_all(x, axis):
    peers = lax.axis_size(axis)
    return lax.all_to_all(jnp.broadcast_to(x[None], (peers, *x.shape)), axis, 0, 0, tiled=True)


def halves(square):
    high = square.astype(BF16).astype(F32)
    return high, (square - high).astype(BF16).astype(F32)


def square_to_tile(square):
    m, n = square.shape
    high, low = halves(square)
    parts = []
    for at in range(0, m, HIGH):
        parts += [high[at : at + HIGH], low[at : at + HIGH]]
    if (spare := LANES - 2 * n * (m // HIGH)) > 0:
        parts.append(jnp.zeros((HIGH, spare), F32))
    return jnp.concatenate(parts, axis=1).astype(BF16)


def tile_to_square(tile, m, n):
    wide = tile.astype(F32)
    rows = []
    for group in range(m // HIGH):
        at = 2 * n * group
        rows.append(wide[:, at : at + n] + wide[:, at + n : at + 2 * n])
    return jnp.concatenate(rows, axis=0)


def places(rows, width):
    return [
        (slice(r, r + HIGH), slice(c, c + LANES))
        for r in range(0, rows, HIGH)
        for c in range(0, width, LANES)
    ]


def from_tiles(ref, part, rows, width):
    across = width // LANES
    return jnp.concatenate(
        [
            jnp.concatenate([ref[part, r * across + c] for c in range(across)], axis=1)
            for r in range(rows // HIGH)
        ],
        axis=0,
    )


def pack_kernel(plane_ref, unused_ref, out_ref):
    rows, width = plane_ref.shape
    two = 2 * rows // 3
    peers = out_ref.shape[0]
    down = plane_ref[two:, :]
    square = square_to_tile(lax.dot_general(down, down, NT, preferred_element_type=F32))
    for at, (r, c) in enumerate(places(two, width)):
        tile = plane_ref[r, c]
        for p in range(peers):
            out_ref[p, at] = tile
    for p in range(peers):
        out_ref[p, out_ref.shape[1] - 1] = square


def token_columns(core, part, parts, width, tok_ref, got_ref):
    columns = pl.ds(pl.multiple_of((core * parts + part) * width, width), width)
    return jnp.concatenate([tok_ref[:, columns], got_ref[:, columns]], axis=0)


def pre_kernel(width, core_ref, tok_ref, got_ref, w_ref, out_ref):
    parts, tiles = w_ref.shape[:2]
    two = (tiles - 1) * HIGH * LANES // width
    hid = two // 2
    core = core_ref[0]
    pre = jnp.zeros((2 * tok_ref.shape[0], two), F32)
    square = jnp.zeros((hid, hid), F32)
    for part in range(parts):
        pre += lax.dot_general(
            token_columns(core, part, parts, width, tok_ref, got_ref),
            from_tiles(w_ref, part, two, width),
            NT,
            preferred_element_type=F32,
        )
        square += tile_to_square(w_ref[part, tiles - 1], hid, hid)
    out_ref[:two, :] = pre.T
    blank = jnp.zeros((hid, out_ref.shape[1] - hid), F32)
    out_ref[two:, :] = jnp.concatenate([square, blank], axis=1)


def grad_kernel(loss_scale, width, parts, core_ref, tok_ref, got_ref, own_ref, other_ref, out_ref):
    peers, tiles = out_ref.shape[:2]
    lanes = peers // parts
    hid = own_ref.shape[0] // 3
    two = 2 * hid
    share = hid // lanes
    toks = tok_ref.shape[0]
    core = core_ref[0]
    other = jnp.concatenate([other_ref[:two, toks:], other_ref[:two, :toks]], axis=1)
    pre = own_ref[:two, :] + other
    high, low = halves(own_ref[two:, :hid] + other_ref[two:, :hid])
    gate_pre = pre[:hid]
    up_pre = pre[hid:]
    sigmoid_gate = jax.nn.sigmoid(gate_pre)
    active = gate_pre * sigmoid_gate
    hidden = (active * up_pre).astype(BF16)
    hidden_grad = loss_scale * (
        jnp.dot(high.astype(BF16), hidden, preferred_element_type=F32)
        + jnp.dot(low.astype(BF16), hidden, preferred_element_type=F32)
    )
    gate_grad = hidden_grad * up_pre * (sigmoid_gate * (1.0 + gate_pre * (1.0 - sigmoid_gate)))
    up_grad = hidden_grad * active
    grads = jnp.concatenate([gate_grad, up_grad], axis=0).astype(BF16)
    square = lax.dot_general(hidden, hidden, NT, preferred_element_type=F32)
    squares = [square_to_tile(square[k * share : (k + 1) * share]) for k in range(lanes)]
    for part in range(parts):
        chip = token_columns(core, part, parts, width, tok_ref, got_ref)
        terms = jnp.dot(grads, chip, preferred_element_type=F32).astype(BF16)
        for lane in range(lanes):
            to = part * lanes + lane
            for at, (r, c) in enumerate(places(2 * share, width)):
                which, row = divmod(r.start, share)
                first = which * hid + lane * share + row
                out_ref[to, at] = terms[first : first + HIGH, c]
            out_ref[to, tiles - 1] = squares[lane]


def sum_kernel(hid, got_ref, out_ref):
    peers, tiles = got_ref.shape[:2]
    rows, width = out_ref.shape
    two = 2 * rows // 3
    share = two // 2
    for at, (r, c) in enumerate(places(two, width)):
        total = got_ref[0, at].astype(F32)
        for p in range(1, peers):
            total += got_ref[p, at].astype(F32)
        out_ref[r, c] = total.astype(BF16)
    square = tile_to_square(got_ref[0, tiles - 1], share, hid)
    for p in range(1, peers):
        square += tile_to_square(got_ref[p, tiles - 1], share, hid)
    blank = jnp.zeros((share, LANES - hid), F32)
    high, low = halves(square)
    both = [jnp.concatenate([half, blank], axis=1).astype(BF16) for half in (high, low)]
    out_ref[two:, : 2 * LANES] = jnp.concatenate(both, axis=1)
    out_ref[two:, 2 * LANES :] = jnp.zeros((share, width - 2 * LANES), BF16)


def final_kernel(loss_scale, kind_ref, got_ref, gathered_ref, out_ref):
    total = got_ref[0].astype(F32)
    for at in range(1, got_ref.shape[0]):
        total += got_ref[at].astype(F32)
    hid = gathered_ref.shape[0] // 3

    @pl.when(kind_ref[0] != 2)
    def _():
        for to in range(out_ref.shape[0]):
            out_ref[to] = total

    @pl.when(kind_ref[0] == 2)
    def _():
        row = (total[0:1] + total[1:2]) * loss_scale
        result = jnp.zeros(total.shape, F32)
        for at in range(hid):
            factor = jnp.broadcast_to(row[:, at : at + 1], total.shape)
            result += factor * gathered_ref[2 * hid + at].astype(F32)
        for to in range(out_ref.shape[0]):
            out_ref[to] = result


def call(kernel, name, shape, dtype, *args):
    return pl.pallas_call(
        kernel,
        out_shape=jax.ShapeDtypeStruct(shape, dtype),
        in_specs=[SMEM if a.dtype == jnp.int32 else VMEM for a in args],
        out_specs=VMEM,
        compiler_params=pltpu.CompilerParams(vmem_limit_bytes=32 << 20),
        name=name,
    )(*args)


def per_device(tokens, gate_weight, up_weight, down_weight):
    xs, cs, yls, zls = (lax.axis_size(a) for a in ("x", "c", "yl", "zl"))
    tok_rows, features = tokens.shape
    hid = lax.axis_size(BLK)
    loss_scale = float(tok_rows * lax.axis_size(AXES)) ** (-0.5)
    width = features // (xs * cs)
    rows = 3 * hid
    tiles = 2 * hid * width // (HIGH * LANES)
    core = lax.axis_index("c")
    kind = lax.axis_index("zl")
    swap = [(i, (i + 1) % cs) for i in range(cs)]

    got_tokens = lax.ppermute(tokens, "c", swap)

    at = (core * xs + lax.axis_index("x")) * width
    mine = lax.select_n(kind, gate_weight, up_weight, down_weight)
    piece = lax.dynamic_slice(mine, (0, at), (1, width)).reshape(ROW_TILE)
    by_place = sent_to_all(piece, PLANE).reshape(*(lax.axis_size(a) for a in PLANE), *ROW_TILE)
    gathered = by_place.transpose(3, 1, 0, 2, 4, 5).reshape(rows, *ROW_TILE)
    packed = pl.pallas_call(
        pack_kernel,
        out_shape=jax.ShapeDtypeStruct((xs, tiles + 1, HIGH, LANES), BF16),
        in_specs=[VMEM, pl.BlockSpec(memory_space=pl.ANY)],
        out_specs=VMEM,
        compiler_params=pltpu.CompilerParams(vmem_limit_bytes=32 << 20),
        name="pack",
    )(gathered.reshape(rows, width), got_tokens)
    weights = lax.all_to_all(packed, "x", 0, 0, tiled=True)

    which = core.reshape(1)
    pre = call(
        lambda *refs: pre_kernel(width, *refs),
        "pre",
        (rows, cs * tok_rows),
        F32,
        which,
        tokens,
        got_tokens,
        weights,
    )
    other = lax.ppermute(pre, "c", swap)
    terms = call(
        lambda *refs: grad_kernel(loss_scale, width, xs, *refs),
        "grad",
        (xs * yls, tiles // yls + 1, HIGH, LANES),
        BF16,
        which,
        tokens,
        got_tokens,
        pre,
        other,
    )
    got = lax.all_to_all(terms, NEAR, 0, 0, tiled=True)
    sums = call(lambda *refs: sum_kernel(hid, *refs), "sums", (rows // yls, width), BF16, got)
    by_kind = sums.reshape(zls, -1, *ROW_TILE).transpose(1, 0, 2, 3).reshape(-1, *ROW_TILE)
    got = lax.all_to_all(by_kind, FAR, 0, 0, tiled=True)
    every = call(
        lambda *refs: final_kernel(loss_scale, *refs),
        "final",
        (xs * zls * cs, *ROW_TILE),
        F32,
        kind.reshape(1),
        got,
        gathered,
    )
    result = lax.all_to_all(every, OWNERS, 0, 0, tiled=True).reshape(zls, 1, features)
    return (result[0], result[1], result[2])


def solution(mesh):
    split = Mesh(mesh.devices.reshape(4, 2, 4, 4, 3, 2), AXES)
    return jax.shard_map(
        per_device,
        mesh=split,
        in_specs=(P(AXES, None), P(BLK, None), P(BLK, None), P(BLK, None)),
        out_specs=(P(BLK, None), P(BLK, None), P(BLK, None)),
        check_vma=False,
    )
```

```python
import jax
import jax.numpy as jnp
from jax import lax
from jax.experimental import pallas as pl
from jax.experimental.pallas import tpu as pltpu
from jax.sharding import Mesh
from jax.sharding import PartitionSpec as P

AXES = ("yh", "yl", "zh", "x", "zl", "c")
BLK = AXES[:3]
PLANE = ("yl", "yh", "zh")
NEAR = ("x", "yl")
FAR = ("zl", "yh", "zh")
OWNERS = ("zl", "c", "x")
ROW_TILE = (8, 128)
HIGH, LANES = 16, 128
NT = (((1,), (1,)), ((), ()))
F32, BF16 = jnp.float32, jnp.bfloat16
VMEM = pl.BlockSpec(memory_space=pltpu.VMEM)
SMEM = pl.BlockSpec(memory_space=pltpu.SMEM)


def sent_to_all(x, axis):
    peers = lax.axis_size(axis)
    return lax.all_to_all(jnp.broadcast_to(x[None], (peers, *x.shape)), axis, 0, 0, tiled=True)


def halves(square):
    high = square.astype(BF16).astype(F32)
    return high, (square - high).astype(BF16).astype(F32)


def square_to_tile(square):
    m, n = square.shape
    high, low = halves(square)
    parts = []
    for at in range(0, m, HIGH):
        parts += [high[at : at + HIGH], low[at : at + HIGH]]
    if (spare := LANES - 2 * n * (m // HIGH)) > 0:
        parts.append(jnp.zeros((HIGH, spare), F32))
    return jnp.concatenate(parts, axis=1).astype(BF16)


def tile_to_square(tile, m, n):
    wide = tile.astype(F32)
    rows = []
    for group in range(m // HIGH):
        at = 2 * n * group
        rows.append(wide[:, at : at + n] + wide[:, at + n : at + 2 * n])
    return jnp.concatenate(rows, axis=0)


def places(rows, width):
    return [
        (slice(r, r + HIGH), slice(c, c + LANES))
        for r in range(0, rows, HIGH)
        for c in range(0, width, LANES)
    ]


def from_tiles(ref, part, rows, width):
    across = width // LANES
    return jnp.concatenate(
        [
            jnp.concatenate([ref[part, r * across + c] for c in range(across)], axis=1)
            for r in range(rows // HIGH)
        ],
        axis=0,
    )


def pack_kernel(plane_ref, unused_ref, out_ref):
    rows, width = plane_ref.shape
    two = 2 * rows // 3
    peers = out_ref.shape[0]
    down = plane_ref[two:, :]
    square = square_to_tile(lax.dot_general(down, down, NT, preferred_element_type=F32))
    for at, (r, c) in enumerate(places(two, width)):
        tile = plane_ref[r, c]
        for p in range(peers):
            out_ref[p, at] = tile
    for p in range(peers):
        out_ref[p, out_ref.shape[1] - 1] = square


def token_columns(core, part, parts, width, tok_ref, got_ref):
    columns = pl.ds(pl.multiple_of((core * parts + part) * width, width), width)
    return jnp.concatenate([tok_ref[:, columns], got_ref[:, columns]], axis=0)


def pre_kernel(width, core_ref, tok_ref, got_ref, w_ref, out_ref):
    parts, tiles = w_ref.shape[:2]
    two = (tiles - 1) * HIGH * LANES // width
    hid = two // 2
    core = core_ref[0]
    pre = jnp.zeros((2 * tok_ref.shape[0], two), F32)
    square = jnp.zeros((hid, hid), F32)
    for part in range(parts):
        pre += lax.dot_general(
            token_columns(core, part, parts, width, tok_ref, got_ref),
            from_tiles(w_ref, part, two, width),
            NT,
            preferred_element_type=F32,
        )
        square += tile_to_square(w_ref[part, tiles - 1], hid, hid)
    out_ref[:two, :] = pre.T
    blank = jnp.zeros((hid, out_ref.shape[1] - hid), F32)
    out_ref[two:, :] = jnp.concatenate([square, blank], axis=1)


def grad_kernel(loss_scale, width, parts, core_ref, tok_ref, got_ref, own_ref, other_ref, out_ref):
    peers, tiles = out_ref.shape[:2]
    lanes = peers // parts
    hid = own_ref.shape[0] // 3
    two = 2 * hid
    share = hid // lanes
    toks = tok_ref.shape[0]
    core = core_ref[0]
    other = jnp.concatenate([other_ref[:two, toks:], other_ref[:two, :toks]], axis=1)
    pre = own_ref[:two, :] + other
    high, low = halves(own_ref[two:, :hid] + other_ref[two:, :hid])
    gate_pre = pre[:hid]
    up_pre = pre[hid:]
    sigmoid_gate = jax.nn.sigmoid(gate_pre)
    active = gate_pre * sigmoid_gate
    hidden = (active * up_pre).astype(BF16)
    hidden_grad = loss_scale * (
        jnp.dot(high.astype(BF16), hidden, preferred_element_type=F32)
        + jnp.dot(low.astype(BF16), hidden, preferred_element_type=F32)
    )
    gate_grad = hidden_grad * up_pre * (sigmoid_gate * (1.0 + gate_pre * (1.0 - sigmoid_gate)))
    up_grad = hidden_grad * active
    grads = jnp.concatenate([gate_grad, up_grad], axis=0).astype(BF16)
    square = lax.dot_general(hidden, hidden, NT, preferred_element_type=F32)
    squares = [square_to_tile(square[k * share : (k + 1) * share]) for k in range(lanes)]
    for part in range(parts):
        chip = token_columns(core, part, parts, width, tok_ref, got_ref)
        terms = jnp.dot(grads, chip, preferred_element_type=F32).astype(BF16)
        for lane in range(lanes):
            to = part * lanes + lane
            for at, (r, c) in enumerate(places(2 * share, width)):
                which, row = divmod(r.start, share)
                first = which * hid + lane * share + row
                out_ref[to, at] = terms[first : first + HIGH, c]
            out_ref[to, tiles - 1] = squares[lane]


def sum_kernel(hid, got_ref, out_ref):
    peers, tiles = got_ref.shape[:2]
    rows, width = out_ref.shape
    two = 2 * rows // 3
    share = two // 2
    for at, (r, c) in enumerate(places(two, width)):
        total = got_ref[0, at].astype(F32)
        for p in range(1, peers):
            total += got_ref[p, at].astype(F32)
        out_ref[r, c] = total.astype(BF16)
    square = tile_to_square(got_ref[0, tiles - 1], share, hid)
    for p in range(1, peers):
        square += tile_to_square(got_ref[p, tiles - 1], share, hid)
    blank = jnp.zeros((share, LANES - hid), F32)
    high, low = halves(square)
    both = [jnp.concatenate([half, blank], axis=1).astype(BF16) for half in (high, low)]
    out_ref[two:, : 2 * LANES] = jnp.concatenate(both, axis=1)
    out_ref[two:, 2 * LANES :] = jnp.zeros((share, width - 2 * LANES), BF16)


def final_kernel(loss_scale, kind_ref, got_ref, gathered_ref, out_ref):
    total = got_ref[0].astype(F32)
    for at in range(1, got_ref.shape[0]):
        total += got_ref[at].astype(F32)
    hid = gathered_ref.shape[0] // 3

    @pl.when(kind_ref[0] != 2)
    def _():
        for to in range(out_ref.shape[0]):
            out_ref[to] = total

    @pl.when(kind_ref[0] == 2)
    def _():
        row = (total[0:1] + total[1:2]) * loss_scale
        result = jnp.zeros(total.shape, F32)
        for at in range(hid):
            factor = jnp.broadcast_to(row[:, at : at + 1], total.shape)
            result += factor * gathered_ref[2 * hid + at].astype(F32)
        for to in range(out_ref.shape[0]):
            out_ref[to] = result


def call(kernel, name, shape, dtype, *args):
    return pl.pallas_call(
        kernel,
        out_shape=jax.ShapeDtypeStruct(shape, dtype),
        in_specs=[SMEM if a.dtype == jnp.int32 else VMEM for a in args],
        out_specs=VMEM,
        compiler_params=pltpu.CompilerParams(vmem_limit_bytes=32 << 20),
        name=name,
    )(*args)


def per_device(tokens, gate_weight, up_weight, down_weight):
    xs, cs, yls, zls = (lax.axis_size(a) for a in ("x", "c", "yl", "zl"))
    tok_rows, features = tokens.shape
    hid = lax.axis_size(BLK)
    loss_scale = float(tok_rows * lax.axis_size(AXES)) ** (-0.5)
    width = features // (xs * cs)
    rows = 3 * hid
    tiles = 2 * hid * width // (HIGH * LANES)
    core = lax.axis_index("c")
    kind = lax.axis_index("zl")
    swap = [(i, (i + 1) % cs) for i in range(cs)]

    got_tokens = lax.ppermute(tokens, "c", swap)

    at = (core * xs + lax.axis_index("x")) * width
    pieces = [
        lax.dynamic_slice(weight, (0, at), (1, width)).reshape(ROW_TILE)
        for weight in (gate_weight, up_weight, down_weight)
    ]
    by_place = sent_to_all(jnp.concatenate(pieces, axis=0), PLANE)
    gathered = by_place.reshape(hid, 3, *ROW_TILE).transpose(1, 0, 2, 3).reshape(rows, *ROW_TILE)
    packed = pl.pallas_call(
        pack_kernel,
        out_shape=jax.ShapeDtypeStruct((xs, tiles + 1, HIGH, LANES), BF16),
        in_specs=[VMEM, pl.BlockSpec(memory_space=pl.ANY)],
        out_specs=VMEM,
        compiler_params=pltpu.CompilerParams(vmem_limit_bytes=32 << 20),
        name="pack",
    )(gathered.reshape(rows, width), got_tokens)
    weights = lax.all_to_all(packed, "x", 0, 0, tiled=True)

    which = core.reshape(1)
    pre = call(
        lambda *refs: pre_kernel(width, *refs),
        "pre",
        (rows, cs * tok_rows),
        F32,
        which,
        tokens,
        got_tokens,
        weights,
    )
    other = lax.ppermute(pre, "c", swap)
    terms = call(
        lambda *refs: grad_kernel(loss_scale, width, xs, *refs),
        "grad",
        (xs * yls, tiles // yls + 1, HIGH, LANES),
        BF16,
        which,
        tokens,
        got_tokens,
        pre,
        other,
    )
    got = lax.all_to_all(terms, NEAR, 0, 0, tiled=True)
    sums = call(lambda *refs: sum_kernel(hid, *refs), "sums", (rows // yls, width), BF16, got)
    got = lax.all_to_all(sums.reshape(-1, *ROW_TILE), FAR, 0, 0, tiled=True)
    every = call(
        lambda *refs: final_kernel(loss_scale, *refs),
        "final",
        (xs * zls * cs, *ROW_TILE),
        F32,
        kind.reshape(1),
        got,
        gathered,
    )
    result = lax.all_to_all(every, OWNERS, 0, 0, tiled=True).reshape(zls, 1, features)
    return (result[0], result[1], result[2])


def solution(mesh):
    split = Mesh(mesh.devices.reshape(4, 2, 4, 4, 3, 2), AXES)
    return jax.shard_map(
        per_device,
        mesh=split,
        in_specs=(P(AXES, None), P(BLK, None), P(BLK, None), P(BLK, None)),
        out_specs=(P(BLK, None), P(BLK, None), P(BLK, None)),
        check_vma=False,
    )
```

```python
import jax
import jax.numpy as jnp
from jax import lax
from jax.experimental import pallas as pl
from jax.experimental.pallas import tpu as pltpu
from jax.sharding import Mesh
from jax.sharding import PartitionSpec as P

AXES = ("yh", "yl", "zh", "x", "zl", "c")
BLK = AXES[:3]
PLANE = ("yl", "yh", "zh")
NEAR = ("x", "yl")
FAR = ("zl", "yh", "zh")
OWNERS = ("zl", "c", "x")
ROW_TILE = (8, 128)
HIGH, LANES = 16, 128
NT = (((1,), (1,)), ((), ()))
F32, BF16 = jnp.float32, jnp.bfloat16
VMEM = pl.BlockSpec(memory_space=pltpu.VMEM)
SMEM = pl.BlockSpec(memory_space=pltpu.SMEM)


def sent_to_all(x, axis):
    peers = lax.axis_size(axis)
    return lax.all_to_all(jnp.broadcast_to(x[None], (peers, *x.shape)), axis, 0, 0, tiled=True)


def halves(square):
    high = square.astype(BF16).astype(F32)
    return high, (square - high).astype(BF16).astype(F32)


def square_to_tile(square):
    m, n = square.shape
    high, low = halves(square)
    parts = []
    for at in range(0, m, HIGH):
        parts += [high[at : at + HIGH], low[at : at + HIGH]]
    if (spare := LANES - 2 * n * (m // HIGH)) > 0:
        parts.append(jnp.zeros((HIGH, spare), F32))
    return jnp.concatenate(parts, axis=1).astype(BF16)


def tile_to_square(tile, m, n):
    wide = tile.astype(F32)
    rows = []
    for group in range(m // HIGH):
        at = 2 * n * group
        rows.append(wide[:, at : at + n] + wide[:, at + n : at + 2 * n])
    return jnp.concatenate(rows, axis=0)


def places(rows, width):
    return [
        (slice(r, r + HIGH), slice(c, c + LANES))
        for r in range(0, rows, HIGH)
        for c in range(0, width, LANES)
    ]


def from_tiles(ref, part, rows, width):
    across = width // LANES
    return jnp.concatenate(
        [
            jnp.concatenate([ref[part, r * across + c] for c in range(across)], axis=1)
            for r in range(rows // HIGH)
        ],
        axis=0,
    )


def pack_kernel(plane_ref, unused_ref, out_ref):
    rows, width = plane_ref.shape
    two = 2 * rows // 3
    peers = out_ref.shape[0]
    down = plane_ref[two:, :]
    square = square_to_tile(lax.dot_general(down, down, NT, preferred_element_type=F32))
    for at, (r, c) in enumerate(places(two, width)):
        tile = plane_ref[r, c]
        for p in range(peers):
            out_ref[p, at] = tile
    for p in range(peers):
        out_ref[p, out_ref.shape[1] - 1] = square


def token_columns(core, part, parts, width, tok_ref, got_ref):
    columns = pl.ds(pl.multiple_of((core * parts + part) * width, width), width)
    return jnp.concatenate([tok_ref[:, columns], got_ref[:, columns]], axis=0)


def pre_kernel(width, core_ref, tok_ref, got_ref, w_ref, out_ref):
    parts, tiles = w_ref.shape[:2]
    two = (tiles - 1) * HIGH * LANES // width
    hid = two // 2
    core = core_ref[0]
    pre = jnp.zeros((2 * tok_ref.shape[0], two), F32)
    square = jnp.zeros((hid, hid), F32)
    for part in range(parts):
        pre += lax.dot_general(
            token_columns(core, part, parts, width, tok_ref, got_ref),
            from_tiles(w_ref, part, two, width),
            NT,
            preferred_element_type=F32,
        )
        square += tile_to_square(w_ref[part, tiles - 1], hid, hid)
    out_ref[:two, :] = pre.T
    blank = jnp.zeros((hid, out_ref.shape[1] - hid), F32)
    out_ref[two:, :] = jnp.concatenate([square, blank], axis=1)


def grad_kernel(loss_scale, width, parts, core_ref, tok_ref, got_ref, own_ref, other_ref, out_ref):
    peers, tiles = out_ref.shape[:2]
    lanes = peers // parts
    hid = own_ref.shape[0] // 3
    two = 2 * hid
    share = hid // lanes
    toks = tok_ref.shape[0]
    core = core_ref[0]
    other = jnp.concatenate([other_ref[:two, toks:], other_ref[:two, :toks]], axis=1)
    pre = own_ref[:two, :] + other
    high, low = halves(own_ref[two:, :hid] + other_ref[two:, :hid])
    gate_pre = pre[:hid]
    up_pre = pre[hid:]
    sigmoid_gate = jax.nn.sigmoid(gate_pre)
    active = gate_pre * sigmoid_gate
    hidden = (active * up_pre).astype(BF16)
    hidden_grad = loss_scale * (
        jnp.dot(high.astype(BF16), hidden, preferred_element_type=F32)
        + jnp.dot(low.astype(BF16), hidden, preferred_element_type=F32)
    )
    gate_grad = hidden_grad * up_pre * (sigmoid_gate * (1.0 + gate_pre * (1.0 - sigmoid_gate)))
    up_grad = hidden_grad * active
    grads = jnp.concatenate([gate_grad, up_grad], axis=0).astype(BF16)
    square = lax.dot_general(hidden, hidden, NT, preferred_element_type=F32)
    squares = [square_to_tile(square[k * share : (k + 1) * share]) for k in range(lanes)]
    for part in range(parts):
        chip = token_columns(core, part, parts, width, tok_ref, got_ref)
        terms = jnp.dot(grads, chip, preferred_element_type=F32).astype(BF16)
        for lane in range(lanes):
            to = part * lanes + lane
            for at, (r, c) in enumerate(places(2 * share, width)):
                which, row = divmod(r.start, share)
                first = which * hid + lane * share + row
                out_ref[to, at] = terms[first : first + HIGH, c]
            out_ref[to, tiles - 1] = squares[lane]


def sum_kernel(hid, got_ref, out_ref):
    peers, tiles = got_ref.shape[:2]
    rows, width = out_ref.shape
    two = 2 * rows // 3
    share = two // 2
    for at, (r, c) in enumerate(places(two, width)):
        total = got_ref[0, at].astype(F32)
        for p in range(1, peers):
            total += got_ref[p, at].astype(F32)
        out_ref[r, c] = total.astype(BF16)
    square = tile_to_square(got_ref[0, tiles - 1], share, hid)
    for p in range(1, peers):
        square += tile_to_square(got_ref[p, tiles - 1], share, hid)
    blank = jnp.zeros((share, LANES - hid), F32)
    high, low = halves(square)
    both = [jnp.concatenate([half, blank], axis=1).astype(BF16) for half in (high, low)]
    out_ref[two:, : 2 * LANES] = jnp.concatenate(both, axis=1)
    out_ref[two:, 2 * LANES :] = jnp.zeros((share, width - 2 * LANES), BF16)


def final_kernel(loss_scale, kind_ref, got_ref, gathered_ref, out_ref):
    total = got_ref[0].astype(F32)
    for at in range(1, got_ref.shape[0]):
        total += got_ref[at].astype(F32)
    hid = gathered_ref.shape[0] // 3

    @pl.when(kind_ref[0] != 2)
    def _():
        for to in range(out_ref.shape[0]):
            out_ref[to] = total

    @pl.when(kind_ref[0] == 2)
    def _():
        row = (total[0:1] + total[1:2]) * loss_scale
        result = jnp.zeros(total.shape, F32)
        for at in range(hid):
            factor = jnp.broadcast_to(row[:, at : at + 1], total.shape)
            result += factor * gathered_ref[2 * hid + at].astype(F32)
        for to in range(out_ref.shape[0]):
            out_ref[to] = result


def call(kernel, name, shape, dtype, *args):
    return pl.pallas_call(
        kernel,
        out_shape=jax.ShapeDtypeStruct(shape, dtype),
        in_specs=[SMEM if a.dtype == jnp.int32 else VMEM for a in args],
        out_specs=VMEM,
        compiler_params=pltpu.CompilerParams(vmem_limit_bytes=32 << 20),
        name=name,
    )(*args)


def per_device(tokens, gate_weight, up_weight, down_weight):
    xs, cs, yls, zls = (lax.axis_size(a) for a in ("x", "c", "yl", "zl"))
    tok_rows, features = tokens.shape
    hid = lax.axis_size(BLK)
    loss_scale = float(tok_rows * lax.axis_size(AXES)) ** (-0.5)
    width = features // (xs * cs)
    rows = 3 * hid
    tiles = 2 * hid * width // (HIGH * LANES)
    core = lax.axis_index("c")
    kind = lax.axis_index("zl").reshape(1)
    swap = [(i, (i + 1) % cs) for i in range(cs)]

    got_tokens = lax.ppermute(tokens, "c", swap)

    at = (core * xs + lax.axis_index("x")) * width
    at, kind = lax.optimization_barrier((at, kind))
    pieces = [
        lax.dynamic_slice(weight, (0, at), (1, width)).reshape(ROW_TILE)
        for weight in (gate_weight, up_weight, down_weight)
    ]
    by_place = sent_to_all(jnp.concatenate(pieces, axis=0), PLANE)
    gathered = by_place.reshape(hid, 3, *ROW_TILE).transpose(1, 0, 2, 3).reshape(rows, *ROW_TILE)
    packed = pl.pallas_call(
        pack_kernel,
        out_shape=jax.ShapeDtypeStruct((xs, tiles + 1, HIGH, LANES), BF16),
        in_specs=[VMEM, pl.BlockSpec(memory_space=pl.ANY)],
        out_specs=VMEM,
        compiler_params=pltpu.CompilerParams(vmem_limit_bytes=32 << 20),
        name="pack",
    )(gathered.reshape(rows, width), got_tokens)
    weights = lax.all_to_all(packed, "x", 0, 0, tiled=True)

    which = core.reshape(1)
    pre = call(
        lambda *refs: pre_kernel(width, *refs),
        "pre",
        (rows, cs * tok_rows),
        F32,
        which,
        tokens,
        got_tokens,
        weights,
    )
    other = lax.ppermute(pre, "c", swap)
    terms = call(
        lambda *refs: grad_kernel(loss_scale, width, xs, *refs),
        "grad",
        (xs * yls, tiles // yls + 1, HIGH, LANES),
        BF16,
        which,
        tokens,
        got_tokens,
        pre,
        other,
    )
    got = lax.all_to_all(terms, NEAR, 0, 0, tiled=True)
    sums = call(lambda *refs: sum_kernel(hid, *refs), "sums", (rows // yls, width), BF16, got)
    got = lax.all_to_all(sums.reshape(-1, *ROW_TILE), FAR, 0, 0, tiled=True)
    every = call(
        lambda *refs: final_kernel(loss_scale, *refs),
        "final",
        (xs * zls * cs, *ROW_TILE),
        F32,
        kind,
        got,
        gathered,
    )
    result = lax.all_to_all(every, OWNERS, 0, 0, tiled=True).reshape(zls, 1, features)
    return (result[0], result[1], result[2])


def solution(mesh):
    split = Mesh(mesh.devices.reshape(4, 2, 4, 4, 3, 2), AXES)
    return jax.shard_map(
        per_device,
        mesh=split,
        in_specs=(P(AXES, None), P(BLK, None), P(BLK, None), P(BLK, None)),
        out_specs=(P(BLK, None), P(BLK, None), P(BLK, None)),
        check_vma=False,
    )
```

```python
import jax
import jax.numpy as jnp
from jax import lax
from jax.experimental import pallas as pl
from jax.experimental.pallas import tpu as pltpu
from jax.sharding import Mesh
from jax.sharding import PartitionSpec as P

AXES = ("yh", "yl", "zh", "x", "zl", "c")
BLK = AXES[:3]
PLANE = ("yl", "yh", "zh")
NEAR = ("x", "yl")
FAR = ("zl", "yh", "zh")
OWNERS = ("zl", "c", "x")
ROW_TILE = (8, 128)
HIGH, LANES = 16, 128
NT = (((1,), (1,)), ((), ()))
F32, BF16 = jnp.float32, jnp.bfloat16
VMEM = pl.BlockSpec(memory_space=pltpu.VMEM)
SMEM = pl.BlockSpec(memory_space=pltpu.SMEM)


def sent_to_all(x, axis):
    peers = lax.axis_size(axis)
    return lax.all_to_all(jnp.broadcast_to(x[None], (peers, *x.shape)), axis, 0, 0, tiled=True)


def halves(square):
    high = square.astype(BF16).astype(F32)
    return high, (square - high).astype(BF16).astype(F32)


def square_to_tile(square):
    m, n = square.shape
    high, low = halves(square)
    parts = []
    for at in range(0, m, HIGH):
        parts += [high[at : at + HIGH], low[at : at + HIGH]]
    if (spare := LANES - 2 * n * (m // HIGH)) > 0:
        parts.append(jnp.zeros((HIGH, spare), F32))
    return jnp.concatenate(parts, axis=1).astype(BF16)


def tile_to_square(tile, m, n):
    wide = tile.astype(F32)
    rows = []
    for group in range(m // HIGH):
        at = 2 * n * group
        rows.append(wide[:, at : at + n] + wide[:, at + n : at + 2 * n])
    return jnp.concatenate(rows, axis=0)


def places(rows, width):
    return [
        (slice(r, r + HIGH), slice(c, c + LANES))
        for r in range(0, rows, HIGH)
        for c in range(0, width, LANES)
    ]


def from_tiles(ref, part, rows, width):
    across = width // LANES
    return jnp.concatenate(
        [
            jnp.concatenate([ref[part, r * across + c] for c in range(across)], axis=1)
            for r in range(rows // HIGH)
        ],
        axis=0,
    )


def pack_kernel(plane_ref, out_ref):
    rows, width = plane_ref.shape
    two = 2 * rows // 3
    peers = out_ref.shape[0]
    down = plane_ref[two:, :]
    square = square_to_tile(lax.dot_general(down, down, NT, preferred_element_type=F32))
    for at, (r, c) in enumerate(places(two, width)):
        tile = plane_ref[r, c]
        for p in range(peers):
            out_ref[p, at] = tile
    for p in range(peers):
        out_ref[p, out_ref.shape[1] - 1] = square


def token_columns(core, part, parts, width, tok_ref, got_ref):
    columns = pl.ds(pl.multiple_of((core * parts + part) * width, width), width)
    return jnp.concatenate([tok_ref[:, columns], got_ref[:, columns]], axis=0)


def pre_kernel(width, core_ref, tok_ref, got_ref, w_ref, out_ref):
    parts, tiles = w_ref.shape[:2]
    two = (tiles - 1) * HIGH * LANES // width
    hid = two // 2
    core = core_ref[0]
    pre = jnp.zeros((2 * tok_ref.shape[0], two), F32)
    square = jnp.zeros((hid, hid), F32)
    for part in range(parts):
        pre += lax.dot_general(
            token_columns(core, part, parts, width, tok_ref, got_ref),
            from_tiles(w_ref, part, two, width),
            NT,
            preferred_element_type=F32,
        )
        square += tile_to_square(w_ref[part, tiles - 1], hid, hid)
    out_ref[:two, :] = pre.T
    blank = jnp.zeros((hid, out_ref.shape[1] - hid), F32)
    out_ref[two:, :] = jnp.concatenate([square, blank], axis=1)


def grad_kernel(loss_scale, width, parts, core_ref, tok_ref, got_ref, own_ref, other_ref, out_ref):
    peers, tiles = out_ref.shape[:2]
    lanes = peers // parts
    hid = own_ref.shape[0] // 3
    two = 2 * hid
    share = hid // lanes
    toks = tok_ref.shape[0]
    core = core_ref[0]
    other = jnp.concatenate([other_ref[:two, toks:], other_ref[:two, :toks]], axis=1)
    pre = own_ref[:two, :] + other
    high, low = halves(own_ref[two:, :hid] + other_ref[two:, :hid])
    gate_pre = pre[:hid]
    up_pre = pre[hid:]
    sigmoid_gate = jax.nn.sigmoid(gate_pre)
    active = gate_pre * sigmoid_gate
    hidden = (active * up_pre).astype(BF16)
    hidden_grad = loss_scale * (
        jnp.dot(high.astype(BF16), hidden, preferred_element_type=F32)
        + jnp.dot(low.astype(BF16), hidden, preferred_element_type=F32)
    )
    gate_grad = hidden_grad * up_pre * (sigmoid_gate * (1.0 + gate_pre * (1.0 - sigmoid_gate)))
    up_grad = hidden_grad * active
    grads = jnp.concatenate([gate_grad, up_grad], axis=0).astype(BF16)
    square = lax.dot_general(hidden, hidden, NT, preferred_element_type=F32)
    squares = [square_to_tile(square[k * share : (k + 1) * share]) for k in range(lanes)]
    for part in range(parts):
        chip = token_columns(core, part, parts, width, tok_ref, got_ref)
        terms = jnp.dot(grads, chip, preferred_element_type=F32).astype(BF16)
        for lane in range(lanes):
            to = part * lanes + lane
            for at, (r, c) in enumerate(places(2 * share, width)):
                which, row = divmod(r.start, share)
                first = which * hid + lane * share + row
                out_ref[to, at] = terms[first : first + HIGH, c]
            out_ref[to, tiles - 1] = squares[lane]


def sum_kernel(hid, got_ref, out_ref):
    peers, tiles = got_ref.shape[:2]
    rows, width = out_ref.shape
    two = 2 * rows // 3
    share = two // 2
    for at, (r, c) in enumerate(places(two, width)):
        total = got_ref[0, at].astype(F32)
        for p in range(1, peers):
            total += got_ref[p, at].astype(F32)
        out_ref[r, c] = total.astype(BF16)
    square = tile_to_square(got_ref[0, tiles - 1], share, hid)
    for p in range(1, peers):
        square += tile_to_square(got_ref[p, tiles - 1], share, hid)
    blank = jnp.zeros((share, LANES - hid), F32)
    high, low = halves(square)
    both = [jnp.concatenate([half, blank], axis=1).astype(BF16) for half in (high, low)]
    out_ref[two:, : 2 * LANES] = jnp.concatenate(both, axis=1)
    out_ref[two:, 2 * LANES :] = jnp.zeros((share, width - 2 * LANES), BF16)


def final_kernel(loss_scale, kind_ref, got_ref, gathered_ref, out_ref):
    total = got_ref[0].astype(F32)
    for at in range(1, got_ref.shape[0]):
        total += got_ref[at].astype(F32)
    hid = gathered_ref.shape[0] // 3

    @pl.when(kind_ref[0] != 2)
    def _():
        for to in range(out_ref.shape[0]):
            out_ref[to] = total

    @pl.when(kind_ref[0] == 2)
    def _():
        row = (total[0:1] + total[1:2]) * loss_scale
        result = jnp.zeros(total.shape, F32)
        for at in range(hid):
            factor = jnp.broadcast_to(row[:, at : at + 1], total.shape)
            result += factor * gathered_ref[2 * hid + at].astype(F32)
        for to in range(out_ref.shape[0]):
            out_ref[to] = result


def call(kernel, name, shape, dtype, *args):
    return pl.pallas_call(
        kernel,
        out_shape=jax.ShapeDtypeStruct(shape, dtype),
        in_specs=[SMEM if a.dtype == jnp.int32 else VMEM for a in args],
        out_specs=VMEM,
        compiler_params=pltpu.CompilerParams(vmem_limit_bytes=32 << 20),
        name=name,
    )(*args)


def per_device(tokens, gate_weight, up_weight, down_weight):
    xs, cs, yls, zls = (lax.axis_size(a) for a in ("x", "c", "yl", "zl"))
    tok_rows, features = tokens.shape
    hid = lax.axis_size(BLK)
    loss_scale = float(tok_rows * lax.axis_size(AXES)) ** (-0.5)
    width = features // (xs * cs)
    rows = 3 * hid
    tiles = 2 * hid * width // (HIGH * LANES)
    core = lax.axis_index("c")
    kind = lax.axis_index("zl").reshape(1)
    swap = [(i, (i + 1) % cs) for i in range(cs)]

    at = (core * xs + lax.axis_index("x")) * width
    at, kind = lax.optimization_barrier((at, kind))
    pieces = [
        lax.dynamic_slice(weight, (0, at), (1, width)).reshape(ROW_TILE)
        for weight in (gate_weight, up_weight, down_weight)
    ]
    by_place = sent_to_all(jnp.concatenate(pieces, axis=0), PLANE)
    by_place, tokens = lax.optimization_barrier((by_place, tokens))
    got_tokens = lax.ppermute(tokens, "c", swap)
    gathered = by_place.reshape(hid, 3, *ROW_TILE).transpose(1, 0, 2, 3).reshape(rows, *ROW_TILE)
    packed = call(
        pack_kernel,
        "pack",
        (xs, tiles + 1, HIGH, LANES),
        BF16,
        gathered.reshape(rows, width),
    )
    weights = lax.all_to_all(packed, "x", 0, 0, tiled=True)

    which = core.reshape(1)
    pre = call(
        lambda *refs: pre_kernel(width, *refs),
        "pre",
        (rows, cs * tok_rows),
        F32,
        which,
        tokens,
        got_tokens,
        weights,
    )
    other = lax.ppermute(pre, "c", swap)
    terms = call(
        lambda *refs: grad_kernel(loss_scale, width, xs, *refs),
        "grad",
        (xs * yls, tiles // yls + 1, HIGH, LANES),
        BF16,
        which,
        tokens,
        got_tokens,
        pre,
        other,
    )
    got = lax.all_to_all(terms, NEAR, 0, 0, tiled=True)
    sums = call(lambda *refs: sum_kernel(hid, *refs), "sums", (rows // yls, width), BF16, got)
    got = lax.all_to_all(sums.reshape(-1, *ROW_TILE), FAR, 0, 0, tiled=True)
    every = call(
        lambda *refs: final_kernel(loss_scale, *refs),
        "final",
        (xs * zls * cs, *ROW_TILE),
        F32,
        kind,
        got,
        gathered,
    )
    result = lax.all_to_all(every, OWNERS, 0, 0, tiled=True).reshape(zls, 1, features)
    return (result[0], result[1], result[2])


def solution(mesh):
    split = Mesh(mesh.devices.reshape(4, 2, 4, 4, 3, 2), AXES)
    return jax.shard_map(
        per_device,
        mesh=split,
        in_specs=(P(AXES, None), P(BLK, None), P(BLK, None), P(BLK, None)),
        out_specs=(P(BLK, None), P(BLK, None), P(BLK, None)),
        check_vma=False,
    )
```

```python
import jax
import jax.numpy as jnp
from jax import lax
from jax.experimental import pallas as pl
from jax.experimental.pallas import tpu as pltpu
from jax.sharding import Mesh
from jax.sharding import PartitionSpec as P

AXES = ("yh", "yl", "zh", "x", "zl", "c")
BLK = AXES[:3]
PLANE = ("yl", "yh", "zh")
NEAR = ("x", "yl")
FAR = ("zl", "yh", "zh")
OWNERS = ("zl", "c", "x")
ROW_TILE = (8, 128)
HIGH, LANES = 16, 128
NT = (((1,), (1,)), ((), ()))
F32, BF16 = jnp.float32, jnp.bfloat16
VMEM = pl.BlockSpec(memory_space=pltpu.VMEM)
SMEM = pl.BlockSpec(memory_space=pltpu.SMEM)


def sent_to_all(x, axis):
    peers = lax.axis_size(axis)
    return lax.all_to_all(jnp.broadcast_to(x[None], (peers, *x.shape)), axis, 0, 0, tiled=True)


def halves(square):
    high = square.astype(BF16).astype(F32)
    return high, (square - high).astype(BF16).astype(F32)


def square_to_tile(square):
    m, n = square.shape
    high, low = halves(square)
    parts = []
    for at in range(0, m, HIGH):
        parts += [high[at : at + HIGH], low[at : at + HIGH]]
    if (spare := LANES - 2 * n * (m // HIGH)) > 0:
        parts.append(jnp.zeros((HIGH, spare), F32))
    return jnp.concatenate(parts, axis=1).astype(BF16)


def tile_to_square(tile, m, n):
    wide = tile.astype(F32)
    rows = []
    for group in range(m // HIGH):
        at = 2 * n * group
        rows.append(wide[:, at : at + n] + wide[:, at + n : at + 2 * n])
    return jnp.concatenate(rows, axis=0)


def places(rows, width):
    return [
        (slice(r, r + HIGH), slice(c, c + LANES))
        for r in range(0, rows, HIGH)
        for c in range(0, width, LANES)
    ]


def from_tiles(ref, part, rows, width):
    across = width // LANES
    return jnp.concatenate(
        [
            jnp.concatenate([ref[part, r * across + c] for c in range(across)], axis=1)
            for r in range(rows // HIGH)
        ],
        axis=0,
    )


def pack_kernel(plane_ref, unused_ref, out_ref):
    rows, width = plane_ref.shape
    two = 2 * rows // 3
    peers = out_ref.shape[0]
    down = plane_ref[two:, :]
    square = square_to_tile(lax.dot_general(down, down, NT, preferred_element_type=F32))
    for at, (r, c) in enumerate(places(two, width)):
        tile = plane_ref[r, c]
        for p in range(peers):
            out_ref[p, at] = tile
    for p in range(peers):
        out_ref[p, out_ref.shape[1] - 1] = square


def token_columns(core, part, parts, width, tok_ref, got_ref):
    columns = pl.ds(pl.multiple_of((core * parts + part) * width, width), width)
    return jnp.concatenate([tok_ref[:, columns], got_ref[:, columns]], axis=0)


def pre_kernel(width, core_ref, tok_ref, got_ref, w_ref, out_ref):
    parts, tiles = w_ref.shape[:2]
    two = (tiles - 1) * HIGH * LANES // width
    hid = two // 2
    core = core_ref[0]
    pre = jnp.zeros((two, 2 * tok_ref.shape[0]), F32)
    square = jnp.zeros((hid, hid), F32)
    for part in range(parts):
        pre += lax.dot_general(
            from_tiles(w_ref, part, two, width),
            token_columns(core, part, parts, width, tok_ref, got_ref),
            NT,
            preferred_element_type=F32,
        )
        square += tile_to_square(w_ref[part, tiles - 1], hid, hid)
    out_ref[:two, :] = pre
    blank = jnp.zeros((hid, out_ref.shape[1] - hid), F32)
    out_ref[two:, :] = jnp.concatenate([square, blank], axis=1)


def grad_kernel(loss_scale, width, parts, core_ref, tok_ref, got_ref, own_ref, other_ref, out_ref):
    peers, tiles = out_ref.shape[:2]
    lanes = peers // parts
    hid = own_ref.shape[0] // 3
    two = 2 * hid
    share = hid // lanes
    toks = tok_ref.shape[0]
    core = core_ref[0]
    other = jnp.concatenate([other_ref[:two, toks:], other_ref[:two, :toks]], axis=1)
    pre = own_ref[:two, :] + other
    high, low = halves(own_ref[two:, :hid] + other_ref[two:, :hid])
    gate_pre = pre[:hid]
    up_pre = pre[hid:]
    sigmoid_gate = jax.nn.sigmoid(gate_pre)
    active = gate_pre * sigmoid_gate
    hidden = (active * up_pre).astype(BF16)
    hidden_grad = loss_scale * (
        jnp.dot(high.astype(BF16), hidden, preferred_element_type=F32)
        + jnp.dot(low.astype(BF16), hidden, preferred_element_type=F32)
    )
    gate_grad = hidden_grad * up_pre * (sigmoid_gate * (1.0 + gate_pre * (1.0 - sigmoid_gate)))
    up_grad = hidden_grad * active
    grads = jnp.concatenate([gate_grad, up_grad], axis=0).astype(BF16)
    square = lax.dot_general(hidden, hidden, NT, preferred_element_type=F32)
    squares = [square_to_tile(square[k * share : (k + 1) * share]) for k in range(lanes)]
    for part in range(parts):
        chip = token_columns(core, part, parts, width, tok_ref, got_ref)
        terms = jnp.dot(grads, chip, preferred_element_type=F32).astype(BF16)
        for lane in range(lanes):
            to = part * lanes + lane
            for at, (r, c) in enumerate(places(2 * share, width)):
                which, row = divmod(r.start, share)
                first = which * hid + lane * share + row
                out_ref[to, at] = terms[first : first + HIGH, c]
            out_ref[to, tiles - 1] = squares[lane]


def sum_kernel(hid, got_ref, out_ref):
    peers, tiles = got_ref.shape[:2]
    rows, width = out_ref.shape
    two = 2 * rows // 3
    share = two // 2
    for at, (r, c) in enumerate(places(two, width)):
        total = got_ref[0, at].astype(F32)
        for p in range(1, peers):
            total += got_ref[p, at].astype(F32)
        out_ref[r, c] = total.astype(BF16)
    square = tile_to_square(got_ref[0, tiles - 1], share, hid)
    for p in range(1, peers):
        square += tile_to_square(got_ref[p, tiles - 1], share, hid)
    blank = jnp.zeros((share, LANES - hid), F32)
    high, low = halves(square)
    both = [jnp.concatenate([half, blank], axis=1).astype(BF16) for half in (high, low)]
    out_ref[two:, : 2 * LANES] = jnp.concatenate(both, axis=1)
    out_ref[two:, 2 * LANES :] = jnp.zeros((share, width - 2 * LANES), BF16)


def final_kernel(loss_scale, kind_ref, got_ref, gathered_ref, out_ref):
    total = got_ref[0].astype(F32)
    for at in range(1, got_ref.shape[0]):
        total += got_ref[at].astype(F32)
    hid = gathered_ref.shape[0] // 3

    @pl.when(kind_ref[0] != 2)
    def _():
        for to in range(out_ref.shape[0]):
            out_ref[to] = total

    @pl.when(kind_ref[0] == 2)
    def _():
        row = (total[0:1] + total[1:2]) * loss_scale
        result = jnp.zeros(total.shape, F32)
        for at in range(hid):
            factor = jnp.broadcast_to(row[:, at : at + 1], total.shape)
            result += factor * gathered_ref[2 * hid + at].astype(F32)
        for to in range(out_ref.shape[0]):
            out_ref[to] = result


def call(kernel, name, shape, dtype, *args):
    return pl.pallas_call(
        kernel,
        out_shape=jax.ShapeDtypeStruct(shape, dtype),
        in_specs=[SMEM if a.dtype == jnp.int32 else VMEM for a in args],
        out_specs=VMEM,
        compiler_params=pltpu.CompilerParams(vmem_limit_bytes=32 << 20),
        name=name,
    )(*args)


def per_device(tokens, gate_weight, up_weight, down_weight):
    xs, cs, yls, zls = (lax.axis_size(a) for a in ("x", "c", "yl", "zl"))
    tok_rows, features = tokens.shape
    hid = lax.axis_size(BLK)
    loss_scale = float(tok_rows * lax.axis_size(AXES)) ** (-0.5)
    width = features // (xs * cs)
    rows = 3 * hid
    tiles = 2 * hid * width // (HIGH * LANES)
    core = lax.axis_index("c")
    kind = lax.axis_index("zl").reshape(1)
    swap = [(i, (i + 1) % cs) for i in range(cs)]

    got_tokens = lax.ppermute(tokens, "c", swap)

    at = (core * xs + lax.axis_index("x")) * width
    at, kind = lax.optimization_barrier((at, kind))
    pieces = [
        lax.dynamic_slice(weight, (0, at), (1, width)).reshape(ROW_TILE)
        for weight in (gate_weight, up_weight, down_weight)
    ]
    by_place = sent_to_all(jnp.concatenate(pieces, axis=0), PLANE)
    gathered = by_place.reshape(hid, 3, *ROW_TILE).transpose(1, 0, 2, 3).reshape(rows, *ROW_TILE)
    packed = pl.pallas_call(
        pack_kernel,
        out_shape=jax.ShapeDtypeStruct((xs, tiles + 1, HIGH, LANES), BF16),
        in_specs=[VMEM, pl.BlockSpec(memory_space=pl.ANY)],
        out_specs=VMEM,
        compiler_params=pltpu.CompilerParams(vmem_limit_bytes=32 << 20),
        name="pack",
    )(gathered.reshape(rows, width), got_tokens)
    weights = lax.all_to_all(packed, "x", 0, 0, tiled=True)

    which = core.reshape(1)
    pre = call(
        lambda *refs: pre_kernel(width, *refs),
        "pre",
        (rows, cs * tok_rows),
        F32,
        which,
        tokens,
        got_tokens,
        weights,
    )
    other = lax.ppermute(pre, "c", swap)
    terms = call(
        lambda *refs: grad_kernel(loss_scale, width, xs, *refs),
        "grad",
        (xs * yls, tiles // yls + 1, HIGH, LANES),
        BF16,
        which,
        tokens,
        got_tokens,
        pre,
        other,
    )
    got = lax.all_to_all(terms, NEAR, 0, 0, tiled=True)
    sums = call(lambda *refs: sum_kernel(hid, *refs), "sums", (rows // yls, width), BF16, got)
    got = lax.all_to_all(sums.reshape(-1, *ROW_TILE), FAR, 0, 0, tiled=True)
    every = call(
        lambda *refs: final_kernel(loss_scale, *refs),
        "final",
        (xs * zls * cs, *ROW_TILE),
        F32,
        kind,
        got,
        gathered,
    )
    result = lax.all_to_all(every, OWNERS, 0, 0, tiled=True).reshape(zls, 1, features)
    return (result[0], result[1], result[2])


def solution(mesh):
    split = Mesh(mesh.devices.reshape(4, 2, 4, 4, 3, 2), AXES)
    return jax.shard_map(
        per_device,
        mesh=split,
        in_specs=(P(AXES, None), P(BLK, None), P(BLK, None), P(BLK, None)),
        out_specs=(P(BLK, None), P(BLK, None), P(BLK, None)),
        check_vma=False,
    )
```

```python
import jax
import jax.numpy as jnp
from jax import lax
from jax.experimental import pallas as pl
from jax.experimental.pallas import tpu as pltpu
from jax.sharding import Mesh
from jax.sharding import PartitionSpec as P

AXES = ("yh", "yl", "zh", "x", "zl", "c")
BLK = AXES[:3]
PLANE = ("yl", "yh", "zh")
NEAR = ("x", "yl")
FAR = ("zl", "yh", "zh")
OWNERS = ("zl", "c", "x")
ROW_TILE = (8, 128)
HIGH, LANES = 16, 128
NT = (((1,), (1,)), ((), ()))
F32, BF16 = jnp.float32, jnp.bfloat16
VMEM = pl.BlockSpec(memory_space=pltpu.VMEM)
SMEM = pl.BlockSpec(memory_space=pltpu.SMEM)


def sent_to_all(x, axis):
    peers = lax.axis_size(axis)
    return lax.all_to_all(jnp.broadcast_to(x[None], (peers, *x.shape)), axis, 0, 0, tiled=True)


def halves(square):
    high = square.astype(BF16).astype(F32)
    return high, (square - high).astype(BF16).astype(F32)


def square_to_tile(square):
    m, n = square.shape
    high, low = halves(square)
    parts = []
    for at in range(0, m, HIGH):
        parts += [high[at : at + HIGH], low[at : at + HIGH]]
    if (spare := LANES - 2 * n * (m // HIGH)) > 0:
        parts.append(jnp.zeros((HIGH, spare), F32))
    return jnp.concatenate(parts, axis=1).astype(BF16)


def tile_to_square(tile, m, n):
    wide = tile.astype(F32)
    rows = []
    for group in range(m // HIGH):
        at = 2 * n * group
        rows.append(wide[:, at : at + n] + wide[:, at + n : at + 2 * n])
    return jnp.concatenate(rows, axis=0)


def places(rows, width):
    return [
        (slice(r, r + HIGH), slice(c, c + LANES))
        for r in range(0, rows, HIGH)
        for c in range(0, width, LANES)
    ]


def from_tiles(ref, part, rows, width):
    across = width // LANES
    return jnp.concatenate(
        [
            jnp.concatenate([ref[part, r * across + c] for c in range(across)], axis=1)
            for r in range(rows // HIGH)
        ],
        axis=0,
    )


def pack_kernel(plane_ref, unused_ref, out_ref):
    rows, width = plane_ref.shape
    two = 2 * rows // 3
    peers = out_ref.shape[0]
    down = plane_ref[two:, :]
    square = square_to_tile(lax.dot_general(down, down, NT, preferred_element_type=F32))
    for at, (r, c) in enumerate(places(two, width)):
        tile = plane_ref[r, c]
        for p in range(peers):
            out_ref[p, at] = tile
    for p in range(peers):
        out_ref[p, out_ref.shape[1] - 1] = square


def token_columns(core, part, parts, width, tok_ref, got_ref):
    columns = pl.ds(pl.multiple_of((core * parts + part) * width, width), width)
    return jnp.concatenate([tok_ref[:, columns], got_ref[:, columns]], axis=0)


def pre_kernel(width, core_ref, tok_ref, got_ref, w_ref, out_ref):
    parts, tiles = w_ref.shape[:2]
    two = (tiles - 1) * HIGH * LANES // width
    hid = two // 2
    core = core_ref[0]
    pre = jnp.zeros((two, 2 * tok_ref.shape[0]), F32)
    square = jnp.zeros((hid, hid), F32)
    for part in range(parts):
        pre += lax.dot_general(
            from_tiles(w_ref, part, two, width),
            token_columns(core, part, parts, width, tok_ref, got_ref),
            NT,
            preferred_element_type=F32,
        )
        square += tile_to_square(w_ref[part, tiles - 1], hid, hid)
    out_ref[:two, :] = pre
    blank = jnp.zeros((hid, out_ref.shape[1] - hid), F32)
    out_ref[two:, :] = jnp.concatenate([square, blank], axis=1)


def grad_kernel(loss_scale, width, parts, core_ref, tok_ref, got_ref, own_ref, other_ref, out_ref):
    peers, tiles = out_ref.shape[:2]
    lanes = peers // parts
    hid = own_ref.shape[0] // 3
    two = 2 * hid
    share = hid // lanes
    toks = tok_ref.shape[0]
    core = core_ref[0]
    other = jnp.concatenate([other_ref[:two, toks:], other_ref[:two, :toks]], axis=1)
    pre = own_ref[:two, :] + other
    high, low = halves(own_ref[two:, :hid] + other_ref[two:, :hid])
    gate_pre = pre[:hid]
    up_pre = pre[hid:]
    sigmoid_gate = jax.nn.sigmoid(gate_pre)
    active = gate_pre * sigmoid_gate
    hidden = (active * up_pre).astype(BF16)
    hidden_grad = loss_scale * (
        jnp.dot(high.astype(BF16), hidden, preferred_element_type=F32)
        + jnp.dot(low.astype(BF16), hidden, preferred_element_type=F32)
    )
    gate_grad = hidden_grad * up_pre * (sigmoid_gate * (1.0 + gate_pre * (1.0 - sigmoid_gate)))
    up_grad = hidden_grad * active
    grads = jnp.concatenate([gate_grad, up_grad], axis=0).astype(BF16)
    square = lax.dot_general(hidden, hidden, NT, preferred_element_type=F32)
    squares = [square_to_tile(square[k * share : (k + 1) * share]) for k in range(lanes)]
    for part in range(parts):
        chip = token_columns(core, part, parts, width, tok_ref, got_ref)
        terms = jnp.dot(grads, chip, preferred_element_type=F32).astype(BF16)
        for lane in range(lanes):
            to = part * lanes + lane
            for at, (r, c) in enumerate(places(2 * share, width)):
                which, row = divmod(r.start, share)
                first = which * hid + lane * share + row
                out_ref[to, at] = terms[first : first + HIGH, c]
            out_ref[to, tiles - 1] = squares[lane]


def sum_kernel(hid, got_ref, out_ref):
    peers, tiles = got_ref.shape[:2]
    rows, width = out_ref.shape
    two = 2 * rows // 3
    share = two // 2
    for at, (r, c) in enumerate(places(two, width)):
        total = got_ref[0, at].astype(F32)
        for p in range(1, peers):
            total += got_ref[p, at].astype(F32)
        out_ref[r, c] = total.astype(BF16)
    square = tile_to_square(got_ref[0, tiles - 1], share, hid)
    for p in range(1, peers):
        square += tile_to_square(got_ref[p, tiles - 1], share, hid)
    blank = jnp.zeros((share, LANES - hid), F32)
    high, low = halves(square)
    both = [jnp.concatenate([half, blank], axis=1).astype(BF16) for half in (high, low)]
    out_ref[two:, : 2 * LANES] = jnp.concatenate(both, axis=1)
    out_ref[two:, 2 * LANES :] = jnp.zeros((share, width - 2 * LANES), BF16)


def final_kernel(loss_scale, kind_ref, got_ref, gathered_ref, out_ref):
    total = got_ref[0].astype(F32)
    for at in range(1, got_ref.shape[0]):
        total += got_ref[at].astype(F32)
    hid = gathered_ref.shape[0] // 3

    @pl.when(kind_ref[0] != 2)
    def _():
        for to in range(out_ref.shape[0]):
            out_ref[to] = total

    @pl.when(kind_ref[0] == 2)
    def _():
        row = (total[0:1] + total[1:2]) * loss_scale
        result = jnp.zeros(total.shape, F32)
        for at in range(hid):
            factor = jnp.broadcast_to(row[:, at : at + 1], total.shape)
            result += factor * gathered_ref[2 * hid + at].astype(F32)
        for to in range(out_ref.shape[0]):
            out_ref[to] = result


def out_kernel(every_ref, *refs):
    outs, sems = refs[:3], refs[3]
    share = every_ref.shape[0] // 3
    copies = [
        pltpu.make_async_copy(every_ref.at[pl.ds(kind * share, share)], out, sems.at[kind])
        for kind, out in enumerate(outs)
    ]
    for copy in copies:
        copy.start()
    for copy in copies:
        copy.wait()


def call(kernel, name, shape, dtype, *args):
    return pl.pallas_call(
        kernel,
        out_shape=jax.ShapeDtypeStruct(shape, dtype),
        in_specs=[SMEM if a.dtype == jnp.int32 else VMEM for a in args],
        out_specs=VMEM,
        compiler_params=pltpu.CompilerParams(vmem_limit_bytes=32 << 20),
        name=name,
    )(*args)


def per_device(tokens, gate_weight, up_weight, down_weight):
    xs, cs, yls, zls = (lax.axis_size(a) for a in ("x", "c", "yl", "zl"))
    tok_rows, features = tokens.shape
    hid = lax.axis_size(BLK)
    loss_scale = float(tok_rows * lax.axis_size(AXES)) ** (-0.5)
    width = features // (xs * cs)
    rows = 3 * hid
    tiles = 2 * hid * width // (HIGH * LANES)
    core = lax.axis_index("c")
    kind = lax.axis_index("zl").reshape(1)
    swap = [(i, (i + 1) % cs) for i in range(cs)]

    got_tokens = lax.ppermute(tokens, "c", swap)

    at = (core * xs + lax.axis_index("x")) * width
    at, kind = lax.optimization_barrier((at, kind))
    pieces = [
        lax.dynamic_slice(weight, (0, at), (1, width)).reshape(ROW_TILE)
        for weight in (gate_weight, up_weight, down_weight)
    ]
    by_place = sent_to_all(jnp.concatenate(pieces, axis=0), PLANE)
    gathered = by_place.reshape(hid, 3, *ROW_TILE).transpose(1, 0, 2, 3).reshape(rows, *ROW_TILE)
    packed = pl.pallas_call(
        pack_kernel,
        out_shape=jax.ShapeDtypeStruct((xs, tiles + 1, HIGH, LANES), BF16),
        in_specs=[VMEM, pl.BlockSpec(memory_space=pl.ANY)],
        out_specs=VMEM,
        compiler_params=pltpu.CompilerParams(vmem_limit_bytes=32 << 20),
        name="pack",
    )(gathered.reshape(rows, width), got_tokens)
    weights = lax.all_to_all(packed, "x", 0, 0, tiled=True)

    which = core.reshape(1)
    pre = call(
        lambda *refs: pre_kernel(width, *refs),
        "pre",
        (rows, cs * tok_rows),
        F32,
        which,
        tokens,
        got_tokens,
        weights,
    )
    other = lax.ppermute(pre, "c", swap)
    terms = call(
        lambda *refs: grad_kernel(loss_scale, width, xs, *refs),
        "grad",
        (xs * yls, tiles // yls + 1, HIGH, LANES),
        BF16,
        which,
        tokens,
        got_tokens,
        pre,
        other,
    )
    got = lax.all_to_all(terms, NEAR, 0, 0, tiled=True)
    sums = call(lambda *refs: sum_kernel(hid, *refs), "sums", (rows // yls, width), BF16, got)
    got = lax.all_to_all(sums.reshape(-1, *ROW_TILE), FAR, 0, 0, tiled=True)
    every = call(
        lambda *refs: final_kernel(loss_scale, *refs),
        "final",
        (xs * zls * cs, *ROW_TILE),
        F32,
        kind,
        got,
        gathered,
    )
    result = lax.all_to_all(every, OWNERS, 0, 0, tiled=True)
    one = jax.ShapeDtypeStruct((xs * cs, *ROW_TILE), F32)
    outs = pl.pallas_call(
        out_kernel,
        out_shape=(one, one, one),
        in_specs=[VMEM],
        out_specs=(pl.BlockSpec(memory_space=pl.ANY),) * 3,
        scratch_shapes=[pltpu.SemaphoreType.DMA((3,))],
        compiler_params=pltpu.CompilerParams(vmem_limit_bytes=32 << 20),
        name="out",
    )(result)
    return tuple(out.reshape(1, features) for out in outs)


def solution(mesh):
    split = Mesh(mesh.devices.reshape(4, 2, 4, 4, 3, 2), AXES)
    return jax.shard_map(
        per_device,
        mesh=split,
        in_specs=(P(AXES, None), P(BLK, None), P(BLK, None), P(BLK, None)),
        out_specs=(P(BLK, None), P(BLK, None), P(BLK, None)),
        check_vma=False,
    )
```
